256 devices in a mesh: seq: 64 (over z, x, core), segment: 4 (over y).
Axes of the slice: x: 4, y: 4, z: 8, core: 2. Of those that a mesh axis runs over, the one named last changes fastest.
Arguments:
- queries: bfloat16 [4, 16384, 2560], P('segment', 'seq')
- keys: bfloat16 [4, 16384, 512], P('segment', 'seq')
- values: bfloat16 [4, 16384, 512], P('segment', 'seq'), may hold values from -6 to 6
- out_proj: bfloat16 [4, 2560, 2560], P('segment', 'seq'), may hold values from -0.5 to 0.5
- hidden_in: bfloat16 [16384, 2560], P('seq'), may hold values from -3 to 3
- vertical: int32 [4, 4, 17], P('segment'), may hold values from 0 to 255, as said below
- slash: int32 [4, 4, 4], P('segment'), may hold values from 1 to 8, as said below
Outputs:
- hidden: bfloat16 [4, 16384, 2560], P('segment', 'seq')
The draws below stay inside these ranges and needn't reach their ends.
Inputs may be any that keep to these rules, and one draw needn't show every extreme that they name: `vertical`: entry 0 of every list is block 0; each other entry lies in the blocks of a different seq index, never index 0, so one seq index holds at most one entry of a list. `slash`: the 4 offsets of one list are distinct.
All inputs are finite; a program needn't handle non-finite values.
Results may differ from the reference program's by a relative error of at most 0.006.
Values may be sent and summed in bfloat16 or wider, within the bound.
A program may use at most 320 MiB of HBM per device.

```python
import math
import jax
import jax.numpy as jnp
from jax import lax

H = 20
G = 4
HEAD = 128
DW = 2560
BLK = 64
NS = 4
TOKENS = 16384
NB_DEV = 4
NBLK = 256
NV = 17
N_SEGMENT = 4


def draw_queries(key, part):
    key = jax.random.fold_in(key, 1)
    shape = (N_SEGMENT, TOKENS, G, H // G, HEAD)
    base = jnp.clip(jax.random.normal(key, shape, jnp.float32), -5.0, 5.0)
    return base.reshape(N_SEGMENT, TOKENS, H * HEAD).astype(jnp.bfloat16)


def draw_keys(key, part):
    key = jax.random.fold_in(key, 2)
    shape = (N_SEGMENT, TOKENS, G, HEAD)
    base = jnp.clip(jax.random.normal(key, shape, jnp.float32), -5.0, 5.0)
    return base.reshape(N_SEGMENT, TOKENS, G * HEAD).astype(jnp.bfloat16)


def draw_vertical(key, part):
    key = jax.random.fold_in(key, 3)
    halves = jax.random.split(key, 2)
    owner_keys = jax.random.split(halves[0], N_SEGMENT * G)
    owner_total = NBLK // NB_DEV - 1

    def pick_owners(one_key):
        return jax.random.permutation(one_key, owner_total)[:NV - 1].astype(jnp.int32) + 1
    owners = jax.vmap(pick_owners)(owner_keys)
    within = jax.random.randint(halves[1], (N_SEGMENT * G, NV - 1), 0, NB_DEV)
    blocks = owners * NB_DEV + within.astype(jnp.int32)
    first = jnp.zeros((N_SEGMENT * G, 1), jnp.int32)
    return jnp.concatenate([first, blocks.astype(jnp.int32)], axis=1).reshape(N_SEGMENT, G, NV)


def draw_slash(key, part):
    key = jax.random.fold_in(key, 4)
    thirds = jax.random.split(key, 3)
    span = 2 * NB_DEV
    list_keys = jax.random.split(thirds[0], N_SEGMENT * G)
    topped_keys = jax.random.split(thirds[1], N_SEGMENT * G)

    def drawn_offsets(one_key):
        return jax.random.permutation(one_key, span)[:NS].astype(jnp.int32) + 1

    def topped_offsets(one_key):
        lower = jax.random.permutation(one_key, span - 1)[:NS - 1].astype(jnp.int32) + 1
        return jnp.concatenate([lower, jnp.full((1,), span, jnp.int32)])
    drawn = jax.vmap(drawn_offsets)(list_keys)
    topped = jax.vmap(topped_offsets)(topped_keys)
    chosen_head = jax.random.randint(thirds[2], (N_SEGMENT, 1), 0, G)
    designated = (jnp.arange(G, dtype=jnp.int32)[None, :] == chosen_head.astype(jnp.int32)).reshape(-1)
    offsets = jnp.where(designated[:, None], topped, drawn)
    return offsets.astype(jnp.int32).reshape(N_SEGMENT, G, NS)


def levels(stream_key, shape, shards, smallest, top_value):
    factor_of = 1.0
    for dim, parts in shards:
        draws = jax.random.uniform(jax.random.fold_in(jax.random.fold_in(stream_key, 6), dim), (parts,), jnp.float32, smallest / len(shards), top_value / len(shards))
        factor_of = factor_of * jnp.repeat(jnp.exp(draws), shape[dim] // parts).reshape((-1,) + (1,) * (len(shape) - 1 - dim))
    return factor_of


def centred(stream_key, shape, spread, most, cuts=(), kind=jnp.bfloat16):
    gain = levels(stream_key, shape, cuts, -0.22, 0.18) if cuts else 1.0
    values = jax.random.normal(stream_key, shape, jnp.float32) * spread * gain
    return jnp.minimum(jnp.maximum(values, -most), most).astype(kind)


def setup_inputs(seed: int = 0) -> dict:
    key_of = jax.random.split(jax.random.key(seed), 8)
    queries = draw_queries(jax.random.fold_in(key_of[7], 71), 0)
    keys = draw_keys(jax.random.fold_in(key_of[7], 71), 0)
    values = centred(key_of[2], (N_SEGMENT, TOKENS, G * HEAD), 1.0, 6.0, ((0, 4), (1, 64)))
    out_proj = centred(key_of[3], (N_SEGMENT, H * HEAD, DW), (H * HEAD // 16) ** -0.5, 0.5, ((0, 4), (1, 64)))
    hidden_in = centred(key_of[4], (TOKENS, DW), 0.5, 3.0, ((0, 64),))
    vertical = draw_vertical(jax.random.fold_in(key_of[7], 71), 0)
    slash = draw_slash(jax.random.fold_in(key_of[7], 71), 0)
    return {"queries": queries, "keys": keys, "values": values, "out_proj": out_proj, "hidden_in": hidden_in, "vertical": vertical, "slash": slash}


def layer_attention(query_layer, key_layer, value_layer, vertical_layer, slash_layer):
    kv_heads = key_layer.shape[1] // HEAD
    group_size = query_layer.shape[1] // HEAD // kv_heads
    block_total = query_layer.shape[0] // BLK
    scale = 1.0 / math.sqrt(HEAD)
    query_blocks = query_layer.reshape(block_total, BLK, kv_heads, group_size, HEAD)
    key_blocks = key_layer.reshape(block_total, BLK, kv_heads, HEAD).transpose(2, 0, 1, 3)
    value_blocks = value_layer.reshape(block_total, BLK, kv_heads, HEAD).transpose(2, 0, 1, 3)
    offsets = jnp.concatenate([jnp.zeros((kv_heads, 1), jnp.int32), slash_layer.astype(jnp.int32)], axis=1)
    positions = jnp.arange(BLK, dtype=jnp.int32)
    causal = positions[:, None] >= positions[None, :]
    tile_count = NS + 1 + vertical_layer.shape[1]
    first_tile = jnp.arange(tile_count, dtype=jnp.int32) == 0
    inner_mask = jnp.logical_or(jnp.logical_not(first_tile)[:, None, None], causal[None])
    inner_mask = inner_mask.transpose(1, 0, 2)

    def pick_rows(source, index_list):
        return source[index_list]

    def one_block(block_index):
        tile_blocks = block_index - offsets
        tile_ok = tile_blocks >= 0
        column_ok = jnp.logical_and(vertical_layer < block_index, jnp.all(vertical_layer[:, :, None] != tile_blocks[:, None, 1:], axis=-1))
        indices = jnp.maximum(jnp.concatenate([tile_blocks, vertical_layer.astype(jnp.int32)], axis=1), 0)
        valid = jnp.concatenate([tile_ok, column_ok], axis=1)
        gathered_keys = jax.vmap(pick_rows)(key_blocks, indices)
        gathered_values = jax.vmap(pick_rows)(value_blocks, indices)
        query_block = query_blocks[block_index]
        scores = jnp.einsum('qgrd,gjkd->grqjk', query_block.astype(jnp.float32), gathered_keys.astype(jnp.float32)) * scale
        full_mask = jnp.logical_and(valid[:, None, None, :, None], inner_mask[None, None])
        scores = jnp.where(full_mask, scores, -jnp.inf)
        row_max = lax.optimization_barrier(jnp.max(scores, axis=(3, 4), keepdims=True))
        expo = jnp.exp(scores - row_max)
        total = lax.optimization_barrier(jnp.sum(expo, axis=(3, 4)))
        rounded = lax.optimization_barrier(expo.astype(jnp.bfloat16))
        numerator = jnp.einsum('grqjk,gjkd->grqd', rounded.astype(jnp.float32), gathered_values.astype(jnp.float32))
        attended = (numerator / total[..., None]).astype(jnp.bfloat16)
        return attended.transpose(2, 0, 1, 3).reshape(BLK, kv_heads * group_size * HEAD)
    result = lax.map(one_block, jnp.arange(block_total, dtype=jnp.int32))
    return result.reshape(block_total * BLK, kv_heads * group_size * HEAD)

def reference(queries, keys, values, out_proj, hidden_in, vertical, slash):
    current = hidden_in
    results = []
    for layer_index in range(N_SEGMENT):
        attention = layer_attention(queries[layer_index], keys[layer_index], values[layer_index], vertical[layer_index], slash[layer_index])
        delta = jnp.dot(attention, out_proj[layer_index], preferred_element_type=jnp.float32)
        current = (current.astype(jnp.float32) + delta).astype(jnp.bfloat16)
        results.append(current)
    return jnp.stack(results)
```

```python
import functools
import math

import jax
import jax.numpy as jnp
from jax import lax
from jax.experimental import pallas as pl
from jax.experimental.pallas import tpu as pltpu
from jax.sharding import PartitionSpec as P

HEAD = 128
BLK = 64
NS = 4
X_CHIPS = 4
CHUNK = 256
SUB = 128
BF16 = jnp.bfloat16
F32 = jnp.float32


def wrap(index, size):
    return lax.rem(index + size, size)


def kernel(
    x_chips, n_segment, nv, group,
    q_ref, k_ref, v_ref, w_ref, hid_ref, vert_ref, slash_ref, out_ref,
    q_buf, own, ext, slots, wbuf, wsend, wland, kall, att, yin, yout, delta,
    swap_send, swap_recv, local_sem, hid_sem, ring_send, ring_recv,
    slash_send, slash_recv, att_send, att_recv, y_send, y_recv, out_send, out_recv,
):
    seq = lax.axis_index("seq")
    seg = lax.axis_index("segment")
    chips = lax.axis_size("seq") // 2
    z_chips = chips // x_chips
    core = lax.rem(seq, 2)
    other = 1 - core
    chip = seq // 2
    z = chip // x_chips
    x = lax.rem(chip, x_chips)
    nb = k_ref.shape[0]
    rows = nb * BLK
    half = q_ref.shape[2] // 2
    kvh = k_ref.shape[2] // 2
    heads = kvh // HEAD
    vk = nv * BLK
    width = vk + (NS + 1) * BLK
    n_chunk = half // CHUNK
    wrows = w_ref.shape[0]

    def at_chip(index):
        return {"seq": index * 2 + core}

    sibling = {"seq": chip * 2 + other}
    x_plus = at_chip(z * x_chips + wrap(x + 1, x_chips))
    x_minus = at_chip(z * x_chips + wrap(x - 1, x_chips))
    z_plus = at_chip(wrap(z + 1, z_chips) * x_chips + x)
    z_minus = at_chip(wrap(z - 1, z_chips) * x_chips + x)
    next_chip = at_chip(wrap(chip + 1, chips))
    prev_chip = at_chip(wrap(chip - 1, chips))
    y_plus = {"segment": wrap(seg + 1, n_segment)}
    y_minus = {"segment": wrap(seg - 1, n_segment)}

    def remote(src, dst, send_sem, recv_sem, device):
        return pltpu.make_async_remote_copy(
            src_ref=src, dst_ref=dst, send_sem=send_sem, recv_sem=recv_sem,
            device_id=device, device_id_type=pl.DeviceIdType.MESH,
        )

    barrier = pltpu.get_barrier_semaphore()
    greeted = (sibling, x_plus, x_minus, z_plus, z_minus, next_chip, prev_chip, y_plus, y_minus)
    for device in greeted:
        pl.semaphore_signal(barrier, inc=1, device_id=device, device_id_type=pl.DeviceIdType.MESH)

    mine_kv = pl.ds(pl.multiple_of(core * kvh, 128), kvh)
    their_kv = pl.ds(pl.multiple_of(other * kvh, 128), kvh)
    mine_cols = pl.ds(pl.multiple_of(core * half, 128), half)
    their_cols = pl.ds(pl.multiple_of(other * half, 128), half)
    own_blocks = pl.ds(core * nb, nb)

    w_theirs = w_ref[:, their_cols].astype(F32)
    pad = wsend.shape[0] - wrows
    if pad:
        w_theirs = jnp.concatenate([w_theirs, jnp.zeros((pad, half), F32)], axis=0)
    wsend[...] = w_theirs.astype(BF16)

    pl.semaphore_wait(barrier, len(greeted))

    pairs = [
        (k_ref.at[:, :, their_kv], k_ref.at[:, :, mine_kv], own.at[own_blocks, :, pl.ds(0, kvh)]),
        (v_ref.at[:, :, their_kv], v_ref.at[:, :, mine_kv], own.at[own_blocks, :, pl.ds(kvh, kvh)]),
        (q_ref.at[:, :, their_cols], q_ref.at[:, :, mine_cols], q_buf.at[own_blocks]),
    ]
    swaps = [
        remote(src, dst, swap_send.at[i], swap_recv.at[i], sibling)
        for i, (src, _, dst) in enumerate(pairs)
    ]
    locals_ = [
        pltpu.make_async_copy(src, dst, local_sem.at[i]) for i, (_, src, dst) in enumerate(pairs)
    ]
    w_swap = remote(wsend, wland, swap_send.at[3], swap_recv.at[3], sibling)
    for i in (0, 1):
        swaps[i].start()
        locals_[i].start()
    w_swap.start()
    swaps[2].start()
    locals_[2].start()

    own_rows = pl.ds(pl.multiple_of(core * rows, 16), rows)
    their_rows = pl.ds(pl.multiple_of(other * rows, 16), rows)

    def hid_copies():
        away = remote(
            hid_ref.at[:, their_cols], yin.at[own_rows], swap_send.at[4], swap_recv.at[4], sibling
        )
        stay = pltpu.make_async_copy(hid_ref.at[:, mine_cols], yin.at[own_rows], hid_sem)
        return away, stay

    @pl.when(seg == 0)
    def _():
        away, stay = hid_copies()
        away.start()
        stay.start()

    for i in (0, 1):
        locals_[i].wait()
        swaps[i].wait()

    slash_copy = remote(own, ext.at[pl.ds(0, 2 * nb)], slash_send, slash_recv, next_chip)
    slash_copy.start()

    for hh in range(heads):
        for o in range(2):
            pick = jnp.int32(0)
            for j in range(nv):
                entry = vert_ref[core * heads + hh, j]
                pick += jnp.where(entry // nb == chip * 2 + o, lax.rem(entry, nb), 0)
            tile = o * nb + pick
            slots[hh, z, x, o, :, 0:HEAD] = own[tile, :, pl.ds(hh * HEAD, HEAD)]
            slots[hh, z, x, o, :, HEAD:] = own[tile, :, pl.ds(kvh + hh * HEAD, HEAD)]

    pending = []

    def ring(n, me, plus, minus, whole, part_of, sem, split):
        last = n // 2

        def message(d, k, part, sending):
            sign, device = ((1, plus), (-1, minus))[d]
            out_at = wrap(me - sign * (k - 1), n)
            in_at = wrap(me - sign * k, n)
            send = ring_send.at[sem, d * 8 + (k - 1) * 2 + max(part, 0)]
            recv = ring_recv.at[sem, d * 8 + (k - 1) * 2 + max(part, 0)]
            view = whole if part < 0 else functools.partial(part_of, part)
            place = view(out_at if sending else in_at)
            return remote(place, place, send, recv, device)

        waited = set()

        def arrive(d, k, part):
            if (d, k, part) not in waited:
                waited.add((d, k, part))
                message(d, k, part, False).wait_recv()

        def parts_of(d, k):
            order = [0, 1] if d == 0 else [1, 0]
            if k == last:
                return order[:1]
            return order if split else [-1]

        for k in range(1, last + 1):
            for d in range(2):
                for part in parts_of(d, k):
                    if k > 1:
                        arrive(d, k - 1, part if split else -1)
                    outgoing = message(d, k, part, True)
                    outgoing.start()
                    pending.append(outgoing)
            yield
        for k in range(1, last + 1):
            for d in range(2):
                for part in parts_of(d, k):
                    arrive(d, k, part)

    def x_then_z(buf, half_of, sem):
        yield from ring(
            x_chips, x, x_plus, x_minus,
            lambda p: buf.at[z, p], lambda h, p: half_of(buf.at[z, p], h), sem, False,
        )
        yield from ring(
            z_chips, z, z_plus, z_minus,
            lambda p: buf.at[p],
            lambda h, p: buf.at[p, pl.ds(h * (x_chips // 2), x_chips // 2)], sem + 1, True,
        )

    def z_then_x(buf, half_of, sem):
        yield from ring(
            z_chips, z, z_plus, z_minus,
            lambda p: buf.at[p, x], lambda h, p: half_of(buf.at[p, x], h), sem, False,
        )
        yield from ring(
            x_chips, x, x_plus, x_minus,
            lambda p: buf.at[:, p],
            lambda h, p: buf.at[pl.ds(h * (z_chips // 2), z_chips // 2), p], sem + 1, True,
        )

    def slot_half(view, h):
        return view.at[h]

    def w_half(view, h):
        return view.at[:, pl.ds(h * (CHUNK // 2), CHUNK // 2)]

    def step(generator, count=1):
        for _ in range(count):
            if next(generator, "end") == "end":
                return False
        return True

    slot_gathers = [x_then_z(slots.at[0], slot_half, 0), z_then_x(slots.at[1], slot_half, 2)]
    for generator in slot_gathers:
        step(generator)

    ext[pl.ds(2 * nb, 2 * nb)] = own[...]
    w_swap.wait()
    w_mine = w_ref[:, mine_cols].astype(F32)
    w_landed = wland[...].astype(F32)[:wrows]
    top = jnp.where(core == 0, w_mine, w_landed)
    bottom = jnp.where(core == 0, w_landed, w_mine)
    w_chip = jnp.concatenate([top, bottom], axis=0).astype(BF16)
    for ch in range(n_chunk):
        wbuf[ch, z, x] = w_chip[:, ch * CHUNK : (ch + 1) * CHUNK]

    w_gathers = [
        (z_then_x if ch % 2 == 0 else x_then_z)(wbuf.at[ch], w_half, 4 + 2 * ch)
        for ch in range(n_chunk)
    ]
    live = list(slot_gathers)
    while live:
        live = [g for g in live if step(g)]
    slash_copy.wait()
    locals_[2].wait()
    swaps[2].wait()

    lane = lax.broadcasted_iota(jnp.int32, (1, width), 1)
    diag_at = vk // 128 * 128
    shift = vk - diag_at
    tile_row = lax.broadcasted_iota(jnp.int32, (group * BLK, 128), 0) % BLK
    tile_col = lax.broadcasted_iota(jnp.int32, (group * BLK, 128), 1) - shift
    future = jnp.logical_and(
        jnp.logical_and(tile_col >= 0, tile_col < BLK), tile_col > tile_row
    )
    scale = math.log2(math.e) / math.sqrt(HEAD)

    def fetch_listed(hh):
        head = core * heads + hh
        for j in range(nv):
            entry = vert_ref[head, j]
            owner = entry // nb
            owner_chip = owner // 2
            kall[hh, pl.ds(j * BLK, BLK), :] = slots[
                hh, owner_chip // x_chips, lax.rem(owner_chip, x_chips), lax.rem(owner, 2)
            ]

    def key_info(hh):
        head = core * heads + hh
        info = jnp.zeros((1, width), jnp.int32)
        for j in range(nv):
            info = jnp.where(lane // BLK == j, vert_ref[head, j], info)
        for i in range(NS):
            info = jnp.where(lane // BLK == nv + 1 + i, slash_ref[head, i], info)
        return info

    def attend(hh, info, b):
        head = core * heads + hh
        block = chip * (2 * nb) + b
        offsets = [slash_ref[head, i] for i in range(NS)]
        for i in range(NS + 1):
            tile = 2 * nb + b - (0 if i == 0 else offsets[i - 1])
            place = pl.ds(vk + i * BLK, BLK)
            kall[hh, place, 0:HEAD] = ext[tile, :, pl.ds(hh * HEAD, HEAD)]
            kall[hh, place, HEAD:] = ext[tile, :, pl.ds(kvh + hh * HEAD, HEAD)]
        query = jnp.concatenate(
            [q_buf[b, :, pl.ds((hh * group + h) * HEAD, HEAD)] for h in range(group)], axis=0
        )
        listed = info < block
        for i in range(NS):
            listed = jnp.logical_and(listed, info != block - offsets[i])
        valid = jnp.logical_or(
            jnp.logical_and(lane < vk, listed), jnp.logical_and(lane >= vk, info <= block)
        )
        bias = jnp.where(valid, 0.0, -jnp.inf).astype(F32)
        scores = lax.dot_general(
            query, kall[hh, :, 0:HEAD], (((1,), (1,)), ((), ())), preferred_element_type=F32
        )
        scores = scores + bias
        diag = jnp.where(future, -jnp.inf, scores[:, diag_at : diag_at + 128])
        scores = jnp.concatenate(
            [scores[:, :diag_at], diag, scores[:, diag_at + 128 :]], axis=1
        )
        row_max = jnp.max(scores, axis=1, keepdims=True)
        expo = jnp.exp2((scores - row_max) * scale)
        total = jnp.sum(expo, axis=1, keepdims=True)
        numerator = jnp.dot(expo.astype(BF16), kall[hh, :, HEAD:], preferred_element_type=F32)
        result = (numerator / total).astype(BF16)
        for h in range(group):
            att[core, b, :, pl.ds((hh * group + h) * HEAD, HEAD)] = result[h * BLK : (h + 1) * BLK]

    parts = 4
    per_part = 2 * nb // parts
    att_copies = []
    live = list(w_gathers)
    for g in live:
        step(g)
    for hh in range(heads):
        fetch_listed(hh)
        info = key_info(hh)
        for part in range(parts):
            live = [g for g in live if step(g)]

            @pl.loop(part * per_part, (part + 1) * per_part)
            def _(b):
                attend(hh, info, b)

            view = att.at[
                core, pl.ds(part * per_part, per_part), :, pl.ds(hh * group * HEAD, group * HEAD)
            ]
            copy = remote(
                view, view, att_send.at[hh * parts + part], att_recv.at[hh * parts + part], sibling
            )
            copy.start()
            att_copies.append(copy)
    while live:
        live = [g for g in live if step(g)]
    for copy in att_copies:
        copy.wait()

    @pl.when(seg == 0)
    def _():
        away, stay = hid_copies()
        away.wait()
        stay.wait()

    subs = 2 * rows // SUB

    def y_copy(ch, r):
        place = (pl.ds(r * SUB, SUB), pl.ds(ch * CHUNK, CHUNK))
        return remote(
            yout.at[place], yin.at[place], y_send.at[ch * subs + r], y_recv.at[ch * subs + r], y_plus
        )

    def out_copies(ch):
        cols = pl.ds(ch * CHUNK, CHUNK)
        to = pl.ds(pl.multiple_of(core * half + ch * CHUNK, 128), CHUNK)
        stay = pltpu.make_async_copy(yout.at[own_rows, cols], out_ref.at[:, to], local_sem.at[3 + ch])
        away = remote(
            yout.at[their_rows, cols], out_ref.at[:, to], out_send.at[ch], out_recv.at[ch], sibling
        )
        return stay, away

    k_half = half
    for ch in range(n_chunk):
        left = wbuf[ch, 0 : z_chips // 2].reshape(k_half, CHUNK)
        right = wbuf[ch, z_chips // 2 :].reshape(k_half, CHUNK)
        delta[...] = jnp.dot(
            att[0].reshape(2 * rows, half), left, preferred_element_type=F32
        ) + jnp.dot(att[1].reshape(2 * rows, half), right, preferred_element_type=F32)
        for r in range(subs):
            @pl.when(seg > 0)
            def _():
                y_copy(ch, r).wait_recv()

            place = (pl.ds(r * SUB, SUB), pl.ds(ch * CHUNK, CHUNK))
            yout[place] = (yin[place].astype(F32) + delta[pl.ds(r * SUB, SUB), :]).astype(BF16)

            @pl.when(seg < n_segment - 1)
            def _():
                y_copy(ch, r).start()

        for copy in out_copies(ch):
            copy.start()

    for ch in range(n_chunk):
        for copy in out_copies(ch):
            copy.wait()

    @pl.when(seg < n_segment - 1)
    def _():
        for ch in range(n_chunk):
            for r in range(subs):
                y_copy(ch, r).wait_send()

    for copy in pending:
        copy.wait_send()


def on_device(x_chips, n_segment, queries, keys, values, out_proj, hidden_in, vertical, slash):
    row_count = queries.shape[1]
    nb = row_count // BLK
    dq = queries.shape[2]
    dkv = keys.shape[2]
    nv = vertical.shape[2]
    group = dq // dkv
    half = dq // 2
    kvh = dkv // 2
    heads = kvh // HEAD
    wrows = out_proj.shape[1]
    chips = lax.axis_size("seq") // 2
    z_chips = chips // x_chips
    n_chunk = half // CHUNK
    subs = 2 * row_count // SUB
    wpad = (wrows + 15) // 16 * 16
    width = (nv + NS + 1) * BLK
    dma = pltpu.SemaphoreType.DMA
    any_space = pl.BlockSpec(memory_space=pl.ANY)
    smem = pl.BlockSpec(memory_space=pltpu.SMEM)
    vmem = pl.BlockSpec(memory_space=pltpu.VMEM)
    out = pl.pallas_call(
        functools.partial(kernel, x_chips, n_segment, nv, group),
        out_shape=jax.ShapeDtypeStruct((row_count, dq), BF16),
        in_specs=[any_space, any_space, any_space, vmem, any_space, smem, smem],
        out_specs=any_space,
        scratch_shapes=[
            pltpu.VMEM((2 * nb, BLK, half), BF16),
            pltpu.VMEM((2 * nb, BLK, 2 * kvh), BF16),
            pltpu.VMEM((4 * nb, BLK, 2 * kvh), BF16),
            pltpu.VMEM((heads, z_chips, x_chips, 2, BLK, 2 * HEAD), BF16),
            pltpu.VMEM((n_chunk, z_chips, x_chips, 2 * wrows, CHUNK), BF16),
            pltpu.VMEM((wpad, half), BF16),
            pltpu.VMEM((wpad, half), BF16),
            pltpu.VMEM((heads, width, 2 * HEAD), BF16),
            pltpu.VMEM((2, 2 * nb, BLK, half), BF16),
            pltpu.VMEM((2 * row_count, half), BF16),
            pltpu.VMEM((2 * row_count, half), BF16),
            pltpu.VMEM((2 * row_count, CHUNK), F32),
            dma((5,)),
            dma((5,)),
            dma((3 + n_chunk,)),
            dma,
            dma((4 + 2 * n_chunk, 16)),
            dma((4 + 2 * n_chunk, 16)),
            dma,
            dma,
            dma((heads * 4,)),
            dma((heads * 4,)),
            dma((n_chunk * subs,)),
            dma((n_chunk * subs,)),
            dma((n_chunk,)),
            dma((n_chunk,)),
        ],
        compiler_params=pltpu.CompilerParams(
            collective_id=0, has_side_effects=True, vmem_limit_bytes=56 * 1024 * 1024
        ),
        name="fused_layer",
    )(
        queries[0].reshape(nb, BLK, dq),
        keys[0].reshape(nb, BLK, dkv),
        values[0].reshape(nb, BLK, dkv),
        out_proj[0],
        hidden_in,
        vertical[0],
        slash[0],
    )
    return out[None]


def solution(mesh, x_chips=X_CHIPS):
    in_specs = (
        P("segment", "seq", None),
        P("segment", "seq", None),
        P("segment", "seq", None),
        P("segment", "seq", None),
        P("seq", None),
        P("segment", None, None),
        P("segment", None, None),
    )
    out_specs = P("segment", "seq", None)
    body = functools.partial(on_device, x_chips, mesh.shape["segment"])
    return jax.shard_map(body, mesh=mesh, in_specs=in_specs, out_specs=out_specs, check_vma=False)
```

```python
import functools
import math

import jax
import jax.numpy as jnp
from jax import lax
from jax.experimental import pallas as pl
from jax.experimental.pallas import tpu as pltpu
from jax.sharding import PartitionSpec as P

HEAD = 128
BLK = 64
NS = 4
X_CHIPS = 4
CHUNK = 256
SUB = 128
BF16 = jnp.bfloat16
F32 = jnp.float32


def wrap(index, size):
    return lax.rem(index + size, size)


def kernel(
    x_chips, n_segment, nv, group,
    q_ref, k_ref, v_ref, w_ref, hid_ref, vert_ref, slash_ref, out_ref,
    q_buf, k_own, v_own, picked, own, ext, row_slots, cand_out, cand_in, home_a, home_b, first_blk, wbuf, wsend, wland, kall, att, yin, yout, delta,
    swap_send, swap_recv, local_sem, hid_sem, ring_send, ring_recv, post_send, post_recv,
    slash_send, slash_recv, first_send, first_recv, att_send, att_recv, y_send, y_recv, out_send, out_recv,
):
    seq = lax.axis_index("seq")
    seg = lax.axis_index("segment")
    chips = lax.axis_size("seq") // 2
    z_chips = chips // x_chips
    core = lax.rem(seq, 2)
    other = 1 - core
    chip = seq // 2
    z = chip // x_chips
    x = lax.rem(chip, x_chips)
    nb = k_ref.shape[0]
    rows = nb * BLK
    half = q_ref.shape[2] // 2
    kvh = k_ref.shape[2] // 2
    heads = kvh // HEAD
    vk = nv * BLK
    width = vk + (NS + 1) * BLK
    n_chunk = half // CHUNK
    wrows = w_ref.shape[0]

    def at_chip(index):
        return {"seq": index * 2 + core}

    sibling = {"seq": chip * 2 + other}
    x_plus = at_chip(z * x_chips + wrap(x + 1, x_chips))
    x_minus = at_chip(z * x_chips + wrap(x - 1, x_chips))
    z_plus = at_chip(wrap(z + 1, z_chips) * x_chips + x)
    z_minus = at_chip(wrap(z - 1, z_chips) * x_chips + x)
    next_chip = at_chip(wrap(chip + 1, chips))
    prev_chip = at_chip(wrap(chip - 1, chips))
    y_plus = {"segment": wrap(seg + 1, n_segment)}
    y_minus = {"segment": wrap(seg - 1, n_segment)}

    def remote(src, dst, send_sem, recv_sem, device):
        return pltpu.make_async_remote_copy(
            src_ref=src, dst_ref=dst, send_sem=send_sem, recv_sem=recv_sem,
            device_id=device, device_id_type=pl.DeviceIdType.MESH,
        )

    barrier = pltpu.get_barrier_semaphore()
    z_peers = [at_chip(wrap(z + d, z_chips) * x_chips + x) for d in range(1, z_chips)]
    x_peers = [at_chip(z * x_chips + wrap(x + d, x_chips)) for d in range(1, x_chips)]
    x_cross = [
        {"seq": (z * x_chips + wrap(x + d, x_chips)) * 2 + other} for d in range(1, x_chips)
    ]
    greeted = [sibling, next_chip, prev_chip, y_plus, y_minus] + z_peers + x_peers + x_cross
    for device in greeted:
        pl.semaphore_signal(barrier, inc=1, device_id=device, device_id_type=pl.DeviceIdType.MESH)

    mine_kv = pl.ds(pl.multiple_of(core * kvh, 128), kvh)
    their_kv = pl.ds(pl.multiple_of(other * kvh, 128), kvh)
    mine_cols = pl.ds(pl.multiple_of(core * half, 128), half)
    their_cols = pl.ds(pl.multiple_of(other * half, 128), half)
    own_blocks = pl.ds(core * nb, nb)
    own_rows = pl.ds(pl.multiple_of(core * rows, 16), rows)
    their_rows = pl.ds(pl.multiple_of(other * rows, 16), rows)

    k_load = pltpu.make_async_copy(k_ref, k_own, local_sem.at[0])
    v_load = pltpu.make_async_copy(v_ref, v_own, local_sem.at[1])
    q_load = pltpu.make_async_copy(q_ref.at[:, :, mine_cols], q_buf.at[own_blocks], local_sem.at[2])
    for copy in (k_load, v_load, q_load):
        copy.start()

    w_theirs = w_ref[:, their_cols].astype(F32)
    pad = wsend.shape[0] - wrows
    if pad:
        w_theirs = jnp.concatenate([w_theirs, jnp.zeros((pad, half), F32)], axis=0)
    wsend[...] = w_theirs.astype(BF16)

    k_load.wait()
    v_load.wait()
    for head in range(2 * heads):
        pick = jnp.int32(0)
        for j in range(nv):
            entry = vert_ref[head, j]
            pick += jnp.where(entry // nb == seq, lax.rem(entry, nb), 0)
        picked[head // heads, head % heads, :, 0:HEAD] = k_own[pick, :, pl.ds(head * HEAD, HEAD)]
        picked[head // heads, head % heads, :, HEAD:] = v_own[pick, :, pl.ds(head * HEAD, HEAD)]
    row_slots[x, core] = picked[core]
    own[own_blocks, :, pl.ds(0, kvh)] = k_own[:, :, mine_kv]
    own[own_blocks, :, pl.ds(kvh, kvh)] = v_own[:, :, mine_kv]

    pl.semaphore_wait(barrier, len(greeted))

    pending = []
    posted = [0]

    def post(src, dst, device):
        i = posted[0]
        posted[0] += 1
        copy = remote(src, dst, post_send.at[i], post_recv.at[i], device)
        copy.start()
        pending.append(copy)
        return copy

    def swap(i, src, dst):
        copy = remote(src, dst, swap_send.at[i], swap_recv.at[i], sibling)
        copy.start()
        return copy

    row_copies = [post(picked.at[other], row_slots.at[x, core], sibling)]
    for d in range(x_chips - 1):
        row_copies.append(post(picked.at[core], row_slots.at[x, core], x_peers[d]))
        row_copies.append(post(picked.at[other], row_slots.at[x, core], x_cross[d]))
    w_swap = swap(3, wsend, wland)
    kv_swaps = [
        swap(0, k_own.at[:, :, their_kv], own.at[own_blocks, :, pl.ds(0, kvh)]),
        swap(1, v_own.at[:, :, their_kv], own.at[own_blocks, :, pl.ds(kvh, kvh)]),
    ]
    q_swap = swap(2, q_ref.at[:, :, their_cols], q_buf.at[own_blocks])

    def hid_copies():
        away = remote(
            hid_ref.at[:, their_cols], yin.at[own_rows], swap_send.at[4], swap_recv.at[4], sibling
        )
        stay = pltpu.make_async_copy(hid_ref.at[:, mine_cols], yin.at[own_rows], hid_sem)
        return away, stay

    @pl.when(seg == 0)
    def _():
        away, stay = hid_copies()
        away.start()
        stay.start()

    def ring(n, me, plus, minus, whole, part_of, sem, split):
        last = n // 2

        def message(d, k, part, sending):
            sign, device = ((1, plus), (-1, minus))[d]
            out_at = wrap(me - sign * (k - 1), n)
            in_at = wrap(me - sign * k, n)
            send = ring_send.at[sem, d * 8 + (k - 1) * 2 + max(part, 0)]
            recv = ring_recv.at[sem, d * 8 + (k - 1) * 2 + max(part, 0)]
            view = whole if part < 0 else functools.partial(part_of, part)
            place = view(out_at if sending else in_at)
            return remote(place, place, send, recv, device)

        waited = set()

        def arrive(d, k, part):
            if (d, k, part) not in waited:
                waited.add((d, k, part))
                message(d, k, part, False).wait_recv()

        def parts_of(d, k):
            order = [0, 1] if d == 0 else [1, 0]
            if k == last:
                return order[:1]
            return order if split else [-1]

        for k in range(1, last + 1):
            for d in range(2):
                for part in parts_of(d, k):
                    if k > 1:
                        arrive(d, k - 1, part if split else -1)
                    outgoing = message(d, k, part, True)
                    outgoing.start()
                    pending.append(outgoing)
            yield
        for k in range(1, last + 1):
            for d in range(2):
                for part in parts_of(d, k):
                    arrive(d, k, part)

    def x_then_z(buf, half_of, sem):
        yield from ring(
            x_chips, x, x_plus, x_minus,
            lambda p: buf.at[z, p], lambda h, p: half_of(buf.at[z, p], h), sem, False,
        )
        yield from ring(
            z_chips, z, z_plus, z_minus,
            lambda p: buf.at[p],
            lambda h, p: buf.at[p, pl.ds(h * (x_chips // 2), x_chips // 2)], sem + 1, True,
        )

    def z_then_x(buf, half_of, sem):
        yield from ring(
            z_chips, z, z_plus, z_minus,
            lambda p: buf.at[p, x], lambda h, p: half_of(buf.at[p, x], h), sem, False,
        )
        yield from ring(
            x_chips, x, x_plus, x_minus,
            lambda p: buf.at[:, p],
            lambda h, p: buf.at[pl.ds(h * (z_chips // 2), z_chips // 2), p], sem + 1, True,
        )

    def w_half(view, h):
        return view.at[:, pl.ds(h * (CHUNK // 2), CHUNK // 2)]

    def step(*generators):
        return [g for g in generators if next(g, "end") != "end"]

    w_swap.wait()
    w_mine = w_ref[:, mine_cols].astype(F32)
    w_landed = wland[...].astype(F32)[:wrows]
    top = jnp.where(core == 0, w_mine, w_landed)
    bottom = jnp.where(core == 0, w_landed, w_mine)
    w_chip = jnp.concatenate([top, bottom], axis=0).astype(BF16)
    for ch in range(n_chunk):
        wbuf[ch, z, x] = w_chip[:, ch * CHUNK : (ch + 1) * CHUNK]
    w_gathers = [
        (x_then_z if ch < 2 else z_then_x)(wbuf.at[ch], w_half, 2 * ch) for ch in range(n_chunk)
    ]
    live_w = set(range(n_chunk))
    w_a = [0, 1]
    w_b = list(range(2, n_chunk))

    def step_w(indices):
        for i in indices:
            if i in live_w and not step(w_gathers[i]):
                live_w.discard(i)

    step_w(w_b + w_a)
    for copy in kv_swaps:
        copy.wait()
    ext[pl.ds(2 * nb, 2 * nb)] = own[...]
    for copy in row_copies:
        copy.wait_recv()

    per_head = nv - 1
    pieces = 2 * heads // x_chips
    for zz in range(z_chips):
        hh = zz * x_chips // per_head
        entry = vert_ref[core * heads + hh, 1 + zz * x_chips - hh * per_head + x]
        owner = entry // nb
        cand_out[zz] = row_slots[lax.rem(owner // 2, x_chips), lax.rem(owner, 2), hh]
    cand_copies = [
        post(cand_out.at[wrap(z + d, z_chips)], cand_in.at[z], z_peers[d - 1])
        for d in range(1, z_chips)
    ]

    def first_copy(d):
        return remote(
            first_blk.at[x], first_blk.at[x], first_send.at[d - 1], first_recv, z_peers[d - 1]
        )

    @pl.when(z == 0)
    def _():
        for i in range(pieces):
            piece = x * pieces + i
            cols = pl.ds(pl.multiple_of(lax.rem(piece, 2) * HEAD, 128), HEAD)
            first_blk[x, i] = row_slots[0, 0, piece // 2, :, cols]
        for d in range(1, z_chips):
            first_copy(d).start()

    cand_in[z] = cand_out[z]
    slash_copy = remote(own, ext.at[pl.ds(0, 2 * nb)], slash_send, slash_recv, next_chip)
    slash_copy.start()
    step_w(w_b + w_a)
    for copy in cand_copies:
        copy.wait_recv()

    home_head = chip // per_head
    home_entry = vert_ref[core * heads + home_head, 1 + lax.rem(chip, per_head)]
    chosen = cand_in[home_entry // (2 * nb * x_chips)]
    cut = home_a.shape[2]
    home_a[z, x] = chosen[:cut]
    home_b[z, x] = chosen[cut:]
    a_first = [post(home_a.at[z, x], home_a.at[z, x], device) for device in z_peers]
    b_first = [post(home_b.at[z, x], home_b.at[z, x], device) for device in x_peers]

    @pl.when(z > 0)
    def _():
        first_copy(1).wait_recv()

    first_x = [post(first_blk.at[x], first_blk.at[x], device) for device in x_peers]
    step_w(w_b + w_a)
    for copy in b_first:
        copy.wait_recv()
    b_second = [post(home_b.at[z], home_b.at[z], device) for device in z_peers]
    for copy in a_first:
        copy.wait_recv()
    a_second = []
    for h in range(heads):
        bundle = home_a.at[pl.ds(h * (z_chips // heads), z_chips // heads), x]
        a_second += [post(bundle, bundle, device) for device in x_peers]
    step_w(w_b)
    for copy in first_x + b_second + a_second:
        copy.wait_recv()

    @pl.when(z == 0)
    def _():
        for d in range(1, z_chips):
            first_copy(d).wait_send()

    slash_copy.wait()
    q_load.wait()
    q_swap.wait()
    step_w(w_a + w_b)

    lane = lax.broadcasted_iota(jnp.int32, (1, width), 1)
    diag_at = vk // 128 * 128
    shift = vk - diag_at
    tile_row = lax.broadcasted_iota(jnp.int32, (group * BLK, 128), 0) % BLK
    tile_col = lax.broadcasted_iota(jnp.int32, (group * BLK, 128), 1) - shift
    future = jnp.logical_and(
        jnp.logical_and(tile_col >= 0, tile_col < BLK), tile_col > tile_row
    )
    scale = math.log2(math.e) / math.sqrt(HEAD)

    def fetch_listed(hh):
        for kv in range(2):
            piece = 2 * hh + kv
            kall[hh, 0:BLK, pl.ds(kv * HEAD, HEAD)] = first_blk[piece // pieces, piece % pieces]
        for j in range(1, nv):
            e = hh * per_head + j - 1
            kall[hh, pl.ds(j * BLK, cut), :] = home_a[e // x_chips, e % x_chips]
            kall[hh, pl.ds(j * BLK + cut, BLK - cut), :] = home_b[e // x_chips, e % x_chips]

    def key_info(hh):
        head = core * heads + hh
        info = jnp.zeros((1, width), jnp.int32)
        for j in range(nv):
            info = jnp.where(lane // BLK == j, vert_ref[head, j], info)
        for i in range(NS):
            info = jnp.where(lane // BLK == nv + 1 + i, slash_ref[head, i], info)
        return info

    def attend(hh, info, b):
        head = core * heads + hh
        block = chip * (2 * nb) + b
        offsets = [slash_ref[head, i] for i in range(NS)]
        for i in range(NS + 1):
            tile = 2 * nb + b - (0 if i == 0 else offsets[i - 1])
            place = pl.ds(vk + i * BLK, BLK)
            kall[hh, place, 0:HEAD] = ext[tile, :, pl.ds(hh * HEAD, HEAD)]
            kall[hh, place, HEAD:] = ext[tile, :, pl.ds(kvh + hh * HEAD, HEAD)]
        query = jnp.concatenate(
            [q_buf[b, :, pl.ds((hh * group + h) * HEAD, HEAD)] for h in range(group)], axis=0
        )
        listed = info < block
        for i in range(NS):
            listed = jnp.logical_and(listed, info != block - offsets[i])
        valid = jnp.logical_or(
            jnp.logical_and(lane < vk, listed), jnp.logical_and(lane >= vk, info <= block)
        )
        bias = jnp.where(valid, 0.0, -jnp.inf).astype(F32)
        scores = lax.dot_general(
            query, kall[hh, :, 0:HEAD], (((1,), (1,)), ((), ())), preferred_element_type=F32
        )
        scores = scores + bias
        diag = jnp.where(future, -jnp.inf, scores[:, diag_at : diag_at + 128])
        scores = jnp.concatenate(
            [scores[:, :diag_at], diag, scores[:, diag_at + 128 :]], axis=1
        )
        row_max = jnp.max(scores, axis=1, keepdims=True)
        expo = jnp.exp2((scores - row_max) * scale)
        total = jnp.sum(expo, axis=1, keepdims=True)
        numerator = jnp.dot(expo.astype(BF16), kall[hh, :, HEAD:], preferred_element_type=F32)
        result = (numerator / total).astype(BF16)
        for h in range(group):
            att[core, b, :, pl.ds((hh * group + h) * HEAD, HEAD)] = result[h * BLK : (h + 1) * BLK]

    parts = 4
    per_part = 2 * nb // parts
    att_copies = []
    for hh in range(heads):
        fetch_listed(hh)
        info = key_info(hh)
        for part in range(parts):
            step_w({2: w_a, 5: w_a, 6: w_b}.get(hh * parts + part, ()))

            @pl.loop(part * per_part, (part + 1) * per_part)
            def _(b):
                attend(hh, info, b)

            view = att.at[
                core, pl.ds(part * per_part, per_part), :, pl.ds(hh * group * HEAD, group * HEAD)
            ]
            copy = remote(
                view, view, att_send.at[hh * parts + part], att_recv.at[hh * parts + part], sibling
            )
            copy.start()
            att_copies.append(copy)
    for copy in att_copies:
        copy.wait()

    @pl.when(seg == 0)
    def _():
        away, stay = hid_copies()
        away.wait()
        stay.wait()

    subs = 2 * rows // SUB

    def y_copy(ch, r):
        place = (pl.ds(r * SUB, SUB), pl.ds(ch * CHUNK, CHUNK))
        return remote(
            yout.at[place], yin.at[place], y_send.at[ch * subs + r], y_recv.at[ch * subs + r], y_plus
        )

    def out_copies(ch):
        cols = pl.ds(ch * CHUNK, CHUNK)
        to = pl.ds(pl.multiple_of(core * half + ch * CHUNK, 128), CHUNK)
        stay = pltpu.make_async_copy(yout.at[own_rows, cols], out_ref.at[:, to], local_sem.at[3 + ch])
        away = remote(
            yout.at[their_rows, cols], out_ref.at[:, to], out_send.at[ch], out_recv.at[ch], sibling
        )
        return stay, away

    k_half = half
    for ch in range(n_chunk):
        while ch in live_w:
            step_w(range(n_chunk))
        left = wbuf[ch, 0 : z_chips // 2].reshape(k_half, CHUNK)
        right = wbuf[ch, z_chips // 2 :].reshape(k_half, CHUNK)
        delta[...] = jnp.dot(
            att[0].reshape(2 * rows, half), left, preferred_element_type=F32
        ) + jnp.dot(att[1].reshape(2 * rows, half), right, preferred_element_type=F32)
        for r in range(subs):
            @pl.when(seg > 0)
            def _():
                y_copy(ch, r).wait_recv()

            place = (pl.ds(r * SUB, SUB), pl.ds(ch * CHUNK, CHUNK))
            yout[place] = (yin[place].astype(F32) + delta[pl.ds(r * SUB, SUB), :]).astype(BF16)

            @pl.when(seg < n_segment - 1)
            def _():
                y_copy(ch, r).start()

        for copy in out_copies(ch):
            copy.start()

    for ch in range(n_chunk):
        for copy in out_copies(ch):
            copy.wait()

    @pl.when(seg < n_segment - 1)
    def _():
        for ch in range(n_chunk):
            for r in range(subs):
                y_copy(ch, r).wait_send()

    for copy in pending:
        copy.wait_send()


def on_device(x_chips, n_segment, queries, keys, values, out_proj, hidden_in, vertical, slash):
    row_count = queries.shape[1]
    nb = row_count // BLK
    dq = queries.shape[2]
    dkv = keys.shape[2]
    nv = vertical.shape[2]
    group = dq // dkv
    half = dq // 2
    kvh = dkv // 2
    heads = kvh // HEAD
    wrows = out_proj.shape[1]
    chips = lax.axis_size("seq") // 2
    z_chips = chips // x_chips
    n_chunk = half // CHUNK
    subs = 2 * row_count // SUB
    n_post = 1 + 3 * (z_chips - 1) + (4 + heads) * (x_chips - 1)
    wpad = (wrows + 15) // 16 * 16
    width = (nv + NS + 1) * BLK
    dma = pltpu.SemaphoreType.DMA
    any_space = pl.BlockSpec(memory_space=pl.ANY)
    smem = pl.BlockSpec(memory_space=pltpu.SMEM)
    vmem = pl.BlockSpec(memory_space=pltpu.VMEM)
    out = pl.pallas_call(
        functools.partial(kernel, x_chips, n_segment, nv, group),
        out_shape=jax.ShapeDtypeStruct((row_count, dq), BF16),
        in_specs=[any_space, any_space, any_space, vmem, any_space, smem, smem],
        out_specs=any_space,
        scratch_shapes=[
            pltpu.VMEM((2 * nb, BLK, half), BF16),
            pltpu.VMEM((nb, BLK, dkv), BF16),
            pltpu.VMEM((nb, BLK, dkv), BF16),
            pltpu.VMEM((2, heads, BLK, 2 * HEAD), BF16),
            pltpu.VMEM((2 * nb, BLK, 2 * kvh), BF16),
            pltpu.VMEM((4 * nb, BLK, 2 * kvh), BF16),
            pltpu.VMEM((x_chips, 2, heads, BLK, 2 * HEAD), BF16),
            pltpu.VMEM((z_chips, BLK, 2 * HEAD), BF16),
            pltpu.VMEM((z_chips, BLK, 2 * HEAD), BF16),
            pltpu.VMEM((z_chips, x_chips, 48, 2 * HEAD), BF16),
            pltpu.VMEM((z_chips, x_chips, 16, 2 * HEAD), BF16),
            pltpu.VMEM((x_chips, 2 * heads // x_chips, BLK, HEAD), BF16),
            pltpu.VMEM((n_chunk, z_chips, x_chips, 2 * wrows, CHUNK), BF16),
            pltpu.VMEM((wpad, half), BF16),
            pltpu.VMEM((wpad, half), BF16),
            pltpu.VMEM((heads, width, 2 * HEAD), BF16),
            pltpu.VMEM((2, 2 * nb, BLK, half), BF16),
            pltpu.VMEM((2 * row_count, half), BF16),
            pltpu.VMEM((2 * row_count, half), BF16),
            pltpu.VMEM((2 * row_count, CHUNK), F32),
            dma((5,)),
            dma((5,)),
            dma((3 + n_chunk,)),
            dma,
            dma((2 * n_chunk, 16)),
            dma((2 * n_chunk, 16)),
            dma((n_post,)),
            dma((n_post,)),
            dma,
            dma,
            dma((z_chips - 1,)),
            dma,
            dma((heads * 4,)),
            dma((heads * 4,)),
            dma((n_chunk * subs,)),
            dma((n_chunk * subs,)),
            dma((n_chunk,)),
            dma((n_chunk,)),
        ],
        compiler_params=pltpu.CompilerParams(
            collective_id=0, has_side_effects=True, vmem_limit_bytes=56 * 1024 * 1024
        ),
        name="fused_layer",
    )(
        queries[0].reshape(nb, BLK, dq),
        keys[0].reshape(nb, BLK, dkv),
        values[0].reshape(nb, BLK, dkv),
        out_proj[0],
        hidden_in,
        vertical[0],
        slash[0],
    )
    return out[None]


def solution(mesh, x_chips=X_CHIPS):
    in_specs = (
        P("segment", "seq", None),
        P("segment", "seq", None),
        P("segment", "seq", None),
        P("segment", "seq", None),
        P("seq", None),
        P("segment", None, None),
        P("segment", None, None),
    )
    out_specs = P("segment", "seq", None)
    body = functools.partial(on_device, x_chips, mesh.shape["segment"])
    return jax.shard_map(body, mesh=mesh, in_specs=in_specs, out_specs=out_specs, check_vma=False)
```

```python
import functools
import math

import jax
import jax.numpy as jnp
from jax import lax
from jax.experimental import pallas as pl
from jax.experimental.pallas import tpu as pltpu
from jax.sharding import PartitionSpec as P

HEAD = 128
BLK = 64
NS = 4
X_CHIPS = 4
CHUNK = 256
SUB = 128
SCHEDULE = {
    0: (5, 6, 7, 8, 9), 2: (0, 1, 2, 3, 4, 5, 6, 7, 8, 9), 3: (5, 6, 7, 8, 9),
    5: (5, 6, 7, 8, 9, 0, 1), 7: (0, 1, 5), 8: (6, 2), 9: (0, 1), 10: (2, 5, 7), 11: (0, 1, 3),
    12: (2, 6, 5, 0), 13: (3, 8, 1, 4), 14: (2, 7, 6), 15: (3, 4, 9), 16: (2, 8, 7), 17: (3, 4),
    19: (4, 9),
}
LEVELS = 4
BF16 = jnp.bfloat16
F32 = jnp.float32


def wrap(index, size):
    return lax.rem(index + size, size)


def kernel(
    x_chips, n_segment, nv, group,
    q_ref, k_ref, v_ref, w_ref, hid_ref, vert_ref, slash_ref, out_ref,
    q_buf, k_own, v_own, picked, own, ext, row_slots, cand_out, cand_in, home_a, home_b, first_blk, wbuf, wsend, wland, kall, att, yin, rin, yout, eout, delta,
    swap_send, swap_recv, local_sem, hid_sem, ring_send, ring_recv, post_send, post_recv,
    slash_send, slash_recv, first_send, first_recv, att_send, att_recv, y_send, y_recv, r_send, r_recv, out_send, out_recv,
):
    seq = lax.axis_index("seq")
    seg = lax.axis_index("segment")
    chips = lax.axis_size("seq") // 2
    z_chips = chips // x_chips
    core = lax.rem(seq, 2)
    other = 1 - core
    chip = seq // 2
    z = chip // x_chips
    x = lax.rem(chip, x_chips)
    nb = k_ref.shape[0]
    rows = nb * BLK
    half = q_ref.shape[2] // 2
    kvh = k_ref.shape[2] // 2
    heads = kvh // HEAD
    n_chunk = half // CHUNK
    wrows = w_ref.shape[0]

    def at_chip(index):
        return {"seq": index * 2 + core}

    sibling = {"seq": chip * 2 + other}
    x_plus = at_chip(z * x_chips + wrap(x + 1, x_chips))
    x_minus = at_chip(z * x_chips + wrap(x - 1, x_chips))
    z_plus = at_chip(wrap(z + 1, z_chips) * x_chips + x)
    z_minus = at_chip(wrap(z - 1, z_chips) * x_chips + x)
    next_chip = at_chip(wrap(chip + 1, chips))
    prev_chip = at_chip(wrap(chip - 1, chips))
    y_plus = {"segment": wrap(seg + 1, n_segment)}
    y_minus = {"segment": wrap(seg - 1, n_segment)}

    def remote(src, dst, send_sem, recv_sem, device):
        return pltpu.make_async_remote_copy(
            src_ref=src, dst_ref=dst, send_sem=send_sem, recv_sem=recv_sem,
            device_id=device, device_id_type=pl.DeviceIdType.MESH,
        )

    barrier = pltpu.get_barrier_semaphore()
    z_peers = [at_chip(wrap(z + d, z_chips) * x_chips + x) for d in range(1, z_chips)]
    x_peers = [at_chip(z * x_chips + wrap(x + d, x_chips)) for d in range(1, x_chips)]
    x_cross = [
        {"seq": (z * x_chips + wrap(x + d, x_chips)) * 2 + other} for d in range(1, x_chips)
    ]
    greeted = [sibling, next_chip, prev_chip, y_plus, y_minus] + z_peers + x_peers + x_cross
    for device in greeted:
        pl.semaphore_signal(barrier, inc=1, device_id=device, device_id_type=pl.DeviceIdType.MESH)

    mine_kv = pl.ds(pl.multiple_of(core * kvh, 128), kvh)
    their_kv = pl.ds(pl.multiple_of(other * kvh, 128), kvh)
    mine_cols = pl.ds(pl.multiple_of(core * half, 128), half)
    their_cols = pl.ds(pl.multiple_of(other * half, 128), half)
    own_blocks = pl.ds(core * nb, nb)
    own_rows = pl.ds(pl.multiple_of(core * rows, 16), rows)
    their_rows = pl.ds(pl.multiple_of(other * rows, 16), rows)

    k_load = pltpu.make_async_copy(k_ref, k_own, local_sem.at[0])
    v_load = pltpu.make_async_copy(v_ref, v_own, local_sem.at[1])
    q_load = pltpu.make_async_copy(q_ref.at[:, :, mine_cols], q_buf.at[own_blocks], local_sem.at[2])
    for copy in (k_load, v_load, q_load):
        copy.start()

    w_theirs = w_ref[:, their_cols].astype(F32)
    pad = wsend.shape[0] - wrows
    if pad:
        w_theirs = jnp.concatenate([w_theirs, jnp.zeros((pad, half), F32)], axis=0)
    wsend[...] = w_theirs.astype(BF16)

    k_load.wait()
    v_load.wait()
    for head in range(2 * heads):
        pick = jnp.int32(0)
        for j in range(nv):
            entry = vert_ref[head, j]
            pick += jnp.where(entry // nb == seq, lax.rem(entry, nb), 0)
        picked[head // heads, head % heads, :, 0:HEAD] = k_own[pick, :, pl.ds(head * HEAD, HEAD)]
        picked[head // heads, head % heads, :, HEAD:] = v_own[pick, :, pl.ds(head * HEAD, HEAD)]
    row_slots[x, core] = picked[core]
    own[own_blocks, :, pl.ds(0, kvh)] = k_own[:, :, mine_kv]
    own[own_blocks, :, pl.ds(kvh, kvh)] = v_own[:, :, mine_kv]

    pl.semaphore_wait(barrier, len(greeted))

    pending = []
    posted = [0]

    def post(src, dst, device):
        i = posted[0]
        posted[0] += 1
        copy = remote(src, dst, post_send.at[i], post_recv.at[i], device)
        copy.start()
        pending.append(copy)
        return copy

    def swap(i, src, dst):
        copy = remote(src, dst, swap_send.at[i], swap_recv.at[i], sibling)
        copy.start()
        return copy

    row_copies = [post(picked.at[other], row_slots.at[x, core], sibling)]
    for d in range(x_chips - 1):
        row_copies.append(post(picked.at[core], row_slots.at[x, core], x_peers[d]))
        row_copies.append(post(picked.at[other], row_slots.at[x, core], x_cross[d]))
    w_swap = swap(3, wsend, wland)
    kv_swaps = [
        swap(0, k_own.at[:, :, their_kv], own.at[own_blocks, :, pl.ds(0, kvh)]),
        swap(1, v_own.at[:, :, their_kv], own.at[own_blocks, :, pl.ds(kvh, kvh)]),
    ]
    q_swap = swap(2, q_ref.at[:, :, their_cols], q_buf.at[own_blocks])

    def hid_copies():
        away = remote(
            hid_ref.at[:, their_cols], yin.at[own_rows], swap_send.at[4], swap_recv.at[4], sibling
        )
        stay = pltpu.make_async_copy(hid_ref.at[:, mine_cols], yin.at[own_rows], hid_sem)
        return away, stay

    @pl.when(seg == 0)
    def _():
        away, stay = hid_copies()
        away.start()
        stay.start()

    def ring(n, me, plus, minus, whole, part_of, sem, split):
        last = n // 2

        def message(d, k, part, sending):
            sign, device = ((1, plus), (-1, minus))[d]
            out_at = wrap(me - sign * (k - 1), n)
            in_at = wrap(me - sign * k, n)
            send = ring_send.at[sem, d * 8 + (k - 1) * 2 + max(part, 0)]
            recv = ring_recv.at[sem, d * 8 + (k - 1) * 2 + max(part, 0)]
            view = whole if part < 0 else functools.partial(part_of, part)
            place = view(out_at if sending else in_at)
            return remote(place, place, send, recv, device)

        waited = set()

        def arrive(d, k, part):
            if (d, k, part) not in waited:
                waited.add((d, k, part))
                message(d, k, part, False).wait_recv()

        def parts_of(d, k):
            order = [0, 1] if d == 0 else [1, 0]
            if k == last:
                return order[:1]
            return order if split else [-1]

        for k in range(1, last + 1):
            for d in range(2):
                for part in parts_of(d, k):
                    if k > 1:
                        arrive(d, k - 1, part if split else -1)
                    outgoing = message(d, k, part, True)
                    outgoing.start()
                    pending.append(outgoing)
            yield
        for k in range(1, last + 1):
            for d in range(2):
                for part in parts_of(d, k):
                    arrive(d, k, part)

    def direct(peers, view, sem):
        copies = []
        for i, device in enumerate(peers):
            copy = remote(view, view, ring_send.at[sem, i], ring_recv.at[sem, i], device)
            copy.start()
            copies.append(copy)
        pending.extend(copies)
        yield
        for copy in copies:
            copy.wait_recv()

    def x_then_z(buf, sem):
        yield from direct(x_peers, buf.at[z, x], sem)
        yield from ring(
            z_chips, z, z_plus, z_minus,
            lambda p: buf.at[p],
            lambda h, p: buf.at[p, pl.ds(h * (x_chips // 2), x_chips // 2)], sem + 1, True,
        )

    def z_then_x(buf, sem):
        yield from ring(
            z_chips, z, z_plus, z_minus,
            lambda p: buf.at[p, x], lambda h, p: w_half(buf.at[p, x], h), sem, False,
        )
        yield from ring(
            x_chips, x, x_plus, x_minus,
            lambda p: buf.at[:, p],
            lambda h, p: buf.at[pl.ds(h * (z_chips // 2), z_chips // 2), p], sem + 1, True,
        )

    def w_half(view, h):
        upper = wrows // 16 * 16 + 16 * (wrows % 16 > 0)
        return view.at[pl.ds(upper * h, (2 * wrows - upper) if h else upper)]

    def step(*generators):
        return [g for g in generators if next(g, "end") != "end"]

    w_swap.wait()
    w_mine = w_ref[:, mine_cols].astype(F32)
    w_landed = wland[...].astype(F32)[:wrows]
    top = jnp.where(core == 0, w_mine, w_landed)
    bottom = jnp.where(core == 0, w_landed, w_mine)
    w_chip = jnp.concatenate([top, bottom], axis=0).astype(BF16)
    for ch in range(n_chunk):
        for i in range(2):
            start = ch * CHUNK + i * (CHUNK // 2)
            wbuf[i, ch, z, x] = w_chip[:, start : start + CHUNK // 2]
    w_gathers = [
        x_then_z(wbuf.at[0, ch], 2 * ch) for ch in range(n_chunk)
    ] + [
        z_then_x(wbuf.at[1, ch], 2 * (n_chunk + ch)) for ch in range(n_chunk)
    ]
    live_w = set(range(2 * n_chunk))

    def step_one(i):
        if i in live_w and not step(w_gathers[i]):
            live_w.discard(i)

    def step_w(point):
        for i in SCHEDULE.get(point, ()):
            step_one(i)

    step_w(0)
    for copy in kv_swaps:
        copy.wait()
    for hh in range(heads):
        ext[hh, pl.ds(2 * nb, 2 * nb), :, 0:HEAD] = own[:, :, pl.ds(hh * HEAD, HEAD)]
        ext[hh, pl.ds(2 * nb, 2 * nb), :, HEAD:] = own[:, :, pl.ds(kvh + hh * HEAD, HEAD)]

    def slash_copy(hh):
        return remote(
            ext.at[hh, pl.ds(2 * nb, 2 * nb)], ext.at[hh, pl.ds(0, 2 * nb)],
            slash_send.at[hh], slash_recv.at[hh], next_chip,
        )

    for hh in range(heads):
        slash_copy(hh).start()
    for copy in row_copies:
        copy.wait_recv()

    per_head = nv - 1
    pieces = 2 * heads // x_chips
    for zz in range(z_chips):
        hh = zz * x_chips // per_head
        entry = vert_ref[core * heads + hh, 1 + zz * x_chips - hh * per_head + x]
        owner = entry // nb
        cand_out[zz] = row_slots[lax.rem(owner // 2, x_chips), lax.rem(owner, 2), hh]
    cand_copies = [
        post(cand_out.at[wrap(z + d, z_chips)], cand_in.at[z], z_peers[d - 1])
        for d in range(1, z_chips)
    ]

    def first_copy(d):
        return remote(
            first_blk.at[x], first_blk.at[x], first_send.at[d - 1], first_recv, z_peers[d - 1]
        )

    @pl.when(z == 0)
    def _():
        for i in range(pieces):
            piece = x * pieces + i
            cols = pl.ds(pl.multiple_of(lax.rem(piece, 2) * HEAD, 128), HEAD)
            first_blk[x, i] = row_slots[0, 0, piece // 2, :, cols]
        for d in range(1, z_chips):
            first_copy(d).start()

    cand_in[z] = cand_out[z]
    step_w(2)
    for copy in cand_copies:
        copy.wait_recv()

    home_head = chip // per_head
    home_entry = vert_ref[core * heads + home_head, 1 + lax.rem(chip, per_head)]
    chosen = cand_in[home_entry // (2 * nb * x_chips)]
    cut = home_a.shape[2]
    home_a[z, x] = chosen[:cut]
    home_b[z, x] = chosen[cut:]
    a_first = [post(home_a.at[z, x], home_a.at[z, x], device) for device in z_peers]
    b_first = [post(home_b.at[z, x], home_b.at[z, x], device) for device in x_peers]

    @pl.when(z > 0)
    def _():
        first_copy(1).wait_recv()

    first_x = [post(first_blk.at[x], first_blk.at[x], device) for device in x_peers]
    step_w(3)
    for copy in b_first:
        copy.wait_recv()
    b_second = [post(home_b.at[z], home_b.at[z], device) for device in z_peers]
    step_w(4)
    for copy in a_first:
        copy.wait_recv()
    a_second = []
    for h in range(heads):
        bundle = home_a.at[pl.ds(h * (z_chips // heads), z_chips // heads), x]
        a_second += [post(bundle, bundle, device) for device in x_peers]
    step_w(5)
    for copy in first_x:
        copy.wait_recv()
    q_load.wait()
    q_swap.wait()

    scale = math.log2(math.e) / math.sqrt(HEAD)
    local = (NS + 2) * BLK
    listed = per_head * BLK
    local_lane = lax.broadcasted_iota(jnp.int32, (1, local), 1) // BLK
    listed_lane = lax.broadcasted_iota(jnp.int32, (1, listed), 1) // BLK
    tile_row = lax.broadcasted_iota(jnp.int32, (group * BLK, 2 * BLK), 0) % BLK
    tile_col = lax.broadcasted_iota(jnp.int32, (group * BLK, 2 * BLK), 1) - BLK
    future = tile_col > tile_row

    def query_of(hh, b):
        return jnp.concatenate(
            [q_buf[b, :, pl.ds((hh * group + h) * HEAD, HEAD)] for h in range(group)], axis=0
        )

    def scores_of(query, keys, bias):
        return lax.dot_general(
            query, keys, (((1,), (1,)), ((), ())), preferred_element_type=F32
        ) + bias

    def hidden_by(valid):
        return jnp.where(valid, 0.0, -jnp.inf).astype(F32)

    def not_slash(entries, block, offsets):
        seen = entries < block
        for offset in offsets:
            seen = jnp.logical_and(seen, entries != block - offset)
        return seen

    def local_info(hh):
        head = core * heads + hh
        info = jnp.where(local_lane == 0, vert_ref[head, 0], 0)
        for i in range(NS):
            info = jnp.where(local_lane == 2 + i, slash_ref[head, i], info)
        return info

    def listed_info(hh):
        head = core * heads + hh
        info = jnp.zeros((1, listed), jnp.int32)
        for j in range(per_head):
            info = jnp.where(listed_lane == j, vert_ref[head, 1 + j], info)
        return info

    def fetch_first(hh):
        for kv in range(2):
            piece = 2 * hh + kv
            kall[hh, pl.ds(listed, BLK), pl.ds(kv * HEAD, HEAD)] = first_blk[
                piece // pieces, piece % pieces
            ]

    def fetch_listed(hh):
        for j in range(per_head):
            e = hh * per_head + j
            kall[hh, pl.ds(j * BLK, cut), 0 : 2 * HEAD] = home_a[e // x_chips, e % x_chips]
            kall[hh, pl.ds(j * BLK + cut, BLK - cut), 0 : 2 * HEAD] = home_b[
                e // x_chips, e % x_chips
            ]

    def attend(hh, info_listed, info_local, b):
        head = core * heads + hh
        block = chip * (2 * nb) + b
        offsets = [slash_ref[head, i] for i in range(NS)]
        for i in range(NS + 1):
            tile = 2 * nb + b - (0 if i == 0 else offsets[i - 1])
            kall[hh, pl.ds(listed + (1 + i) * BLK, BLK), 0 : 2 * HEAD] = ext[hh, tile]
        first_seen = jnp.logical_and(local_lane == 0, not_slash(info_local, block, offsets))
        bias = jnp.concatenate(
            [
                hidden_by(not_slash(info_listed, block, offsets)),
                hidden_by(
                    jnp.logical_or(
                        first_seen, jnp.logical_and(local_lane > 0, info_local <= block)
                    )
                ),
            ],
            axis=1,
        )
        scores = scores_of(query_of(hh, b), kall[hh, :, 0:HEAD], bias)
        scores = jnp.concatenate(
            [
                scores[:, :listed],
                jnp.where(future, -jnp.inf, scores[:, listed : listed + 2 * BLK]),
                scores[:, listed + 2 * BLK :],
            ],
            axis=1,
        )
        top = jnp.max(scores, axis=1, keepdims=True)
        expo = jnp.exp2((scores - top) * scale).astype(BF16)
        sums = jnp.dot(expo, kall[hh, :, HEAD:], preferred_element_type=F32)
        result = (sums[:, :HEAD] / sums[:, HEAD:]).astype(BF16)
        for h in range(group):
            att[core, b, :, pl.ds((hh * group + h) * HEAD, HEAD)] = result[h * BLK : (h + 1) * BLK]

    for hh in range(heads):
        kall[hh, :, 2 * HEAD :] = jnp.ones((listed + local, HEAD), BF16)
        fetch_first(hh)
    step_w(7)
    for copy in b_second + a_second:
        copy.wait_recv()

    @pl.when(z == 0)
    def _():
        for d in range(1, z_chips):
            first_copy(d).wait_send()

    step_w(8)
    parts = 4
    per_part = 2 * nb // parts
    att_copies = []
    for hh in range(heads):
        slash_copy(hh).wait_recv()
    for hh in range(heads):
        fetch_listed(hh)
        infos = (listed_info(hh), local_info(hh))
        for part in range(parts):
            step_w(9 + hh * parts + part)

            @pl.loop(part * per_part, (part + 1) * per_part, unroll=2)
            def _(b):
                attend(hh, *infos, b)

            view = att.at[
                core, pl.ds(part * per_part, per_part), :, pl.ds(hh * group * HEAD, group * HEAD)
            ]
            copy = remote(
                view, view, att_send.at[hh * parts + part], att_recv.at[hh * parts + part], sibling
            )
            copy.start()
            att_copies.append(copy)
    step_w(17)
    for copy in att_copies:
        copy.wait()

    @pl.when(seg == 0)
    def _():
        away, stay = hid_copies()
        away.wait()
        stay.wait()

    subs = 2 * rows // SUB

    def piece(ch, r):
        return (pl.ds(r * SUB, SUB), pl.ds(ch * CHUNK, CHUNK))

    def up(ch, r, src):
        at, i = piece(ch, r), ch * subs + r
        return remote(src.at[at], yin.at[at], y_send.at[i], y_recv.at[i], y_plus)

    def down(ch, r, src):
        at, i = piece(ch, r), ch * subs + r
        return remote(src.at[at], rin.at[at], r_send.at[i], r_recv.at[i], y_minus)

    sent = [[] for _ in range(n_segment)]

    def hand_on(level, ch, k):
        def value(buf, r):
            return buf[piece(ch, r)].astype(F32)

        def own_delta(r):
            return delta[ch, pl.ds(r * SUB, SUB), :]

        def store(buf, r, result):
            buf[piece(ch, r)] = result.astype(BF16)

        def go(way, r, src):
            way(ch, r, src).start()
            sent[k].append((way, ch, r, src))

        def come(way, r):
            way(ch, r, yout).wait_recv()

        chain, skip01, skip12, skip23 = range(4)
        if (level, k) == (0, 0):
            for r, way in ((skip01, down), (skip12, up), (skip23, up), (chain, up)):
                store(yout, r, value(yin, r) + own_delta(r))
                go(way, r, yout)
        elif (level, k) == (0, 1):
            for r, way in ((skip12, down), (skip01, up)):
                store(eout, r, own_delta(r))
                go(way, r, eout)
        elif (level, k) == (0, 2):
            for r, way in ((skip23, down), (skip12, up)):
                store(eout, r, own_delta(r))
                go(way, r, eout)
        elif (level, k) == (1, 0):
            come(down, skip12)
            store(eout, skip12, value(yout, skip12) + value(rin, skip12))
            go(down, skip12, eout)
        elif (level, k) == (1, 1):
            come(down, skip23)
            store(eout, skip23, own_delta(skip23) + value(rin, skip23))
            go(down, skip23, eout)
            for r in (skip12, skip23, chain):
                come(up, r)
                store(yout, r, value(yin, r) + own_delta(r))
                if r != skip12:
                    go(up, r, yout)
        elif (level, k) == (1, 2):
            come(up, skip01)
            store(eout, skip01, value(yin, skip01) + own_delta(skip01))
            go(up, skip01, eout)
        elif (level, k) == (1, 3):
            come(down, skip01)
            go(down, skip01, rin)
        elif (level, k) == (2, 0):
            come(down, skip23)
            store(eout, skip23, value(yout, skip23) + value(rin, skip23))
            go(down, skip23, eout)
        elif (level, k) == (2, 2):
            come(down, skip01)
            go(down, skip01, rin)
            store(
                yout, skip01, value(rin, skip01) + value(yin, skip01) + own_delta(skip01)
            )
            for r in (skip23, chain):
                come(up, r)
                store(yout, r, value(yin, r) + own_delta(r))
                if r == chain:
                    go(up, r, yout)
        elif (level, k) == (2, 3):
            come(down, skip12)
            go(down, skip12, rin)
            for r in (skip01, skip12):
                come(up, r)
                store(yout, r, value(rin, r) + value(yin, r) + own_delta(r))
        elif (level, k) == (3, 1):
            come(down, skip01)
            store(yout, skip01, value(rin, skip01) + own_delta(skip01))
        elif (level, k) == (3, 2):
            come(down, skip12)
            store(yout, skip12, value(rin, skip12) + own_delta(skip12))
        elif (level, k) == (3, 3):
            come(down, skip23)
            store(yout, skip23, value(rin, skip23) + own_delta(skip23))
            come(up, chain)
            store(yout, chain, value(yin, chain) + own_delta(chain))

    def out_copies(ch):
        cols = pl.ds(pl.multiple_of(ch * CHUNK, 128), CHUNK)
        to = pl.ds(pl.multiple_of(core * half + ch * CHUNK, 128), CHUNK)
        stay = pltpu.make_async_copy(yout.at[own_rows, cols], out_ref.at[:, to], local_sem.at[3 + ch])
        away = remote(
            yout.at[their_rows, cols], out_ref.at[:, to], out_send.at[ch], out_recv.at[ch], sibling
        )
        return stay, away

    def project(ch):
        step_w(18 + ch)
        while ch in live_w or n_chunk + ch in live_w:
            step_one(ch)
            step_one(n_chunk + ch)
        left, right = (
            jnp.concatenate(
                [
                    wbuf[i, ch, k * z_chips // 2 : (k + 1) * z_chips // 2].reshape(half, CHUNK // 2)
                    for i in range(2)
                ],
                axis=1,
            )
            for k in range(2)
        )
        delta[ch] = jnp.dot(
            att[0].reshape(2 * rows, half), left, preferred_element_type=F32
        ) + jnp.dot(att[1].reshape(2 * rows, half), right, preferred_element_type=F32)

    for t in range(n_chunk + LEVELS - 1):
        if t < n_chunk:
            project(t)
        for level in range(LEVELS):
            ch = t - level
            if 0 <= ch < n_chunk:
                for k in range(n_segment):
                    pl.when(seg == k)(functools.partial(hand_on, level, ch, k))
                if level == LEVELS - 1:
                    for copy in out_copies(ch):
                        copy.start()

    for ch in range(n_chunk):
        for copy in out_copies(ch):
            copy.wait()

    for k in range(n_segment):
        @pl.when(seg == k)
        def _():
            for way, ch, r, src in sent[k]:
                way(ch, r, src).wait_send()

    for copy in pending + [slash_copy(hh) for hh in range(heads)]:
        copy.wait_send()


def on_device(x_chips, n_segment, queries, keys, values, out_proj, hidden_in, vertical, slash):
    row_count = queries.shape[1]
    nb = row_count // BLK
    dq = queries.shape[2]
    dkv = keys.shape[2]
    nv = vertical.shape[2]
    group = dq // dkv
    half = dq // 2
    kvh = dkv // 2
    heads = kvh // HEAD
    wrows = out_proj.shape[1]
    chips = lax.axis_size("seq") // 2
    z_chips = chips // x_chips
    n_chunk = half // CHUNK
    subs = 2 * row_count // SUB
    n_post = 1 + 3 * (z_chips - 1) + (4 + heads) * (x_chips - 1)
    wpad = (wrows + 15) // 16 * 16
    dma = pltpu.SemaphoreType.DMA
    any_space = pl.BlockSpec(memory_space=pl.ANY)
    smem = pl.BlockSpec(memory_space=pltpu.SMEM)
    vmem = pl.BlockSpec(memory_space=pltpu.VMEM)
    out = pl.pallas_call(
        functools.partial(kernel, x_chips, n_segment, nv, group),
        out_shape=jax.ShapeDtypeStruct((row_count, dq), BF16),
        in_specs=[any_space, any_space, any_space, vmem, any_space, smem, smem],
        out_specs=any_space,
        scratch_shapes=[
            pltpu.VMEM((2 * nb, BLK, half), BF16),
            pltpu.VMEM((nb, BLK, dkv), BF16),
            pltpu.VMEM((nb, BLK, dkv), BF16),
            pltpu.VMEM((2, heads, BLK, 2 * HEAD), BF16),
            pltpu.VMEM((2 * nb, BLK, 2 * kvh), BF16),
            pltpu.VMEM((heads, 4 * nb, BLK, 2 * HEAD), BF16),
            pltpu.VMEM((x_chips, 2, heads, BLK, 2 * HEAD), BF16),
            pltpu.VMEM((z_chips, BLK, 2 * HEAD), BF16),
            pltpu.VMEM((z_chips, BLK, 2 * HEAD), BF16),
            pltpu.VMEM((z_chips, x_chips, 48, 2 * HEAD), BF16),
            pltpu.VMEM((z_chips, x_chips, 16, 2 * HEAD), BF16),
            pltpu.VMEM((x_chips, 2 * heads // x_chips, BLK, HEAD), BF16),
            pltpu.VMEM((2, n_chunk, z_chips, x_chips, 2 * wrows, CHUNK // 2), BF16),
            pltpu.VMEM((wpad, half), BF16),
            pltpu.VMEM((wpad, half), BF16),
            pltpu.VMEM((heads, (nv + NS + 1) * BLK, 3 * HEAD), BF16),
            pltpu.VMEM((2, 2 * nb, BLK, half), BF16),
            pltpu.VMEM((2 * row_count, half), BF16),
            pltpu.VMEM((2 * row_count, half), BF16),
            pltpu.VMEM((2 * row_count, half), BF16),
            pltpu.VMEM((2 * row_count, half), BF16),
            pltpu.VMEM((n_chunk, 2 * row_count, CHUNK), F32),
            dma((5,)),
            dma((5,)),
            dma((3 + n_chunk,)),
            dma,
            dma((4 * n_chunk, 16)),
            dma((4 * n_chunk, 16)),
            dma((n_post,)),
            dma((n_post,)),
            dma((heads,)),
            dma((heads,)),
            dma((z_chips - 1,)),
            dma,
            dma((heads * 4,)),
            dma((heads * 4,)),
            dma((n_chunk * subs,)),
            dma((n_chunk * subs,)),
            dma((n_chunk * subs,)),
            dma((n_chunk * subs,)),
            dma((n_chunk,)),
            dma((n_chunk,)),
        ],
        compiler_params=pltpu.CompilerParams(
            collective_id=0, has_side_effects=True, vmem_limit_bytes=56 * 1024 * 1024
        ),
        name="fused_layer",
    )(
        queries[0].reshape(nb, BLK, dq),
        keys[0].reshape(nb, BLK, dkv),
        values[0].reshape(nb, BLK, dkv),
        out_proj[0],
        hidden_in,
        vertical[0],
        slash[0],
    )
    return out[None]


def solution(mesh, x_chips=X_CHIPS):
    in_specs = (
        P("segment", "seq", None),
        P("segment", "seq", None),
        P("segment", "seq", None),
        P("segment", "seq", None),
        P("seq", None),
        P("segment", None, None),
        P("segment", None, None),
    )
    out_specs = P("segment", "seq", None)
    body = functools.partial(on_device, x_chips, mesh.shape["segment"])
    return jax.shard_map(body, mesh=mesh, in_specs=in_specs, out_specs=out_specs, check_vma=False)
```

```python
import functools
import math

import jax
import jax.numpy as jnp
from jax import lax
from jax.experimental import pallas as pl
from jax.experimental.pallas import tpu as pltpu
from jax.sharding import PartitionSpec as P

HEAD = 128
BLK = 64
NS = 4
X_CHIPS = 4
CHUNK = 256
SUB = 128
SCHEDULE = {
    0: (11,), 2: (10, 11), 3: (11,), 5: (10, 11, 0, 1), 7: (11, 0, 1, 5), 8: (6, 2), 9: (0, 1),
    10: (2, 5, 7), 11: (0, 1, 3), 12: (2, 6, 5, 0), 13: (3, 8, 1, 4), 14: (2, 7, 6), 15: (3, 4, 9),
    16: (2, 8, 7), 17: (3, 4), 19: (4, 9),
}
LEVELS = 4
BF16 = jnp.bfloat16
F32 = jnp.float32


def wrap(index, size):
    return lax.rem(index + size, size)


def kernel(
    x_chips, n_segment, nv, group,
    q_ref, k_ref, v_ref, w_ref, hid_ref, vert_ref, slash_ref, out_ref,
    q_buf, k_own, v_own, picked, own, ext, row_slots, cand_out, cand_in, home_a, home_b, first_blk, wbuf, wsend, wland, kall, att, yin, rin, yout, eout, delta,
    swap_send, swap_recv, local_sem, hid_sem, ring_send, ring_recv, post_send, post_recv,
    slash_send, slash_recv, first_send, first_recv, att_send, att_recv, y_send, y_recv, r_send, r_recv, out_send, out_recv,
):
    seq = lax.axis_index("seq")
    seg = lax.axis_index("segment")
    chips = lax.axis_size("seq") // 2
    z_chips = chips // x_chips
    core = lax.rem(seq, 2)
    other = 1 - core
    chip = seq // 2
    z = chip // x_chips
    x = lax.rem(chip, x_chips)
    nb = k_ref.shape[0]
    rows = nb * BLK
    half = q_ref.shape[2] // 2
    kvh = k_ref.shape[2] // 2
    heads = kvh // HEAD
    n_chunk = half // CHUNK
    wrows = w_ref.shape[0]

    def at_chip(index):
        return {"seq": index * 2 + core}

    sibling = {"seq": chip * 2 + other}
    x_plus = at_chip(z * x_chips + wrap(x + 1, x_chips))
    x_minus = at_chip(z * x_chips + wrap(x - 1, x_chips))
    z_plus = at_chip(wrap(z + 1, z_chips) * x_chips + x)
    z_minus = at_chip(wrap(z - 1, z_chips) * x_chips + x)
    next_chip = at_chip(wrap(chip + 1, chips))
    prev_chip = at_chip(wrap(chip - 1, chips))
    y_plus = {"segment": wrap(seg + 1, n_segment)}
    y_minus = {"segment": wrap(seg - 1, n_segment)}

    def remote(src, dst, send_sem, recv_sem, device):
        return pltpu.make_async_remote_copy(
            src_ref=src, dst_ref=dst, send_sem=send_sem, recv_sem=recv_sem,
            device_id=device, device_id_type=pl.DeviceIdType.MESH,
        )

    barrier = pltpu.get_barrier_semaphore()
    z_peers = [at_chip(wrap(z + d, z_chips) * x_chips + x) for d in range(1, z_chips)]
    x_peers = [at_chip(z * x_chips + wrap(x + d, x_chips)) for d in range(1, x_chips)]
    x_cross = [
        {"seq": (z * x_chips + wrap(x + d, x_chips)) * 2 + other} for d in range(1, x_chips)
    ]
    greeted = [sibling, next_chip, prev_chip, y_plus, y_minus] + z_peers + x_peers + x_cross
    for device in greeted:
        pl.semaphore_signal(barrier, inc=1, device_id=device, device_id_type=pl.DeviceIdType.MESH)

    mine_kv = pl.ds(pl.multiple_of(core * kvh, 128), kvh)
    their_kv = pl.ds(pl.multiple_of(other * kvh, 128), kvh)
    mine_cols = pl.ds(pl.multiple_of(core * half, 128), half)
    their_cols = pl.ds(pl.multiple_of(other * half, 128), half)
    own_blocks = pl.ds(core * nb, nb)
    own_rows = pl.ds(pl.multiple_of(core * rows, 16), rows)
    their_rows = pl.ds(pl.multiple_of(other * rows, 16), rows)

    k_load = pltpu.make_async_copy(k_ref, k_own, local_sem.at[0])
    v_load = pltpu.make_async_copy(v_ref, v_own, local_sem.at[1])
    q_load = pltpu.make_async_copy(q_ref.at[:, :, mine_cols], q_buf.at[own_blocks], local_sem.at[2])
    for copy in (k_load, v_load, q_load):
        copy.start()

    w_theirs = w_ref[:, their_cols].astype(F32)
    pad = wsend.shape[0] - wrows
    if pad:
        w_theirs = jnp.concatenate([w_theirs, jnp.zeros((pad, half), F32)], axis=0)
    wsend[...] = w_theirs.astype(BF16)

    k_load.wait()
    v_load.wait()
    for head in range(2 * heads):
        pick = jnp.int32(0)
        for j in range(nv):
            entry = vert_ref[head, j]
            pick += jnp.where(entry // nb == seq, lax.rem(entry, nb), 0)
        picked[head // heads, head % heads, :, 0:HEAD] = k_own[pick, :, pl.ds(head * HEAD, HEAD)]
        picked[head // heads, head % heads, :, HEAD:] = v_own[pick, :, pl.ds(head * HEAD, HEAD)]
    row_slots[x, core] = picked[core]
    own[own_blocks, :, pl.ds(0, kvh)] = k_own[:, :, mine_kv]
    own[own_blocks, :, pl.ds(kvh, kvh)] = v_own[:, :, mine_kv]

    pl.semaphore_wait(barrier, len(greeted))

    pending = []
    posted = [0]

    def post(src, dst, device):
        i = posted[0]
        posted[0] += 1
        copy = remote(src, dst, post_send.at[i], post_recv.at[i], device)
        copy.start()
        pending.append(copy)
        return copy

    def swap(i, src, dst):
        copy = remote(src, dst, swap_send.at[i], swap_recv.at[i], sibling)
        copy.start()
        return copy

    row_copies = [post(picked.at[other], row_slots.at[x, core], sibling)]
    for d in range(x_chips - 1):
        row_copies.append(post(picked.at[core], row_slots.at[x, core], x_peers[d]))
        row_copies.append(post(picked.at[other], row_slots.at[x, core], x_cross[d]))
    w_swap = swap(3, wsend, wland)
    kv_swaps = [
        swap(0, k_own.at[:, :, their_kv], own.at[own_blocks, :, pl.ds(0, kvh)]),
        swap(1, v_own.at[:, :, their_kv], own.at[own_blocks, :, pl.ds(kvh, kvh)]),
    ]
    q_swap = swap(2, q_ref.at[:, :, their_cols], q_buf.at[own_blocks])

    def hid_copies():
        away = remote(
            hid_ref.at[:, their_cols], yin.at[own_rows], swap_send.at[4], swap_recv.at[4], sibling
        )
        stay = pltpu.make_async_copy(hid_ref.at[:, mine_cols], yin.at[own_rows], hid_sem)
        return away, stay

    @pl.when(seg == 0)
    def _():
        away, stay = hid_copies()
        away.start()
        stay.start()

    def ring(n, me, plus, minus, whole, part_of, sem, split):
        last = n // 2

        def message(d, k, part, sending):
            sign, device = ((1, plus), (-1, minus))[d]
            out_at = wrap(me - sign * (k - 1), n)
            in_at = wrap(me - sign * k, n)
            send = ring_send.at[sem, d * 8 + (k - 1) * 2 + max(part, 0)]
            recv = ring_recv.at[sem, d * 8 + (k - 1) * 2 + max(part, 0)]
            view = whole if part < 0 else functools.partial(part_of, part)
            place = view(out_at if sending else in_at)
            return remote(place, place, send, recv, device)

        waited = set()

        def arrive(d, k, part):
            if (d, k, part) not in waited:
                waited.add((d, k, part))
                message(d, k, part, False).wait_recv()

        def parts_of(d, k):
            order = [0, 1] if d == 0 else [1, 0]
            if k == last:
                return order[:1]
            return order if split else [-1]

        for k in range(1, last + 1):
            for d in range(2):
                for part in parts_of(d, k):
                    if k > 1:
                        arrive(d, k - 1, part if split else -1)
                    outgoing = message(d, k, part, True)
                    outgoing.start()
                    pending.append(outgoing)
            yield
        for k in range(1, last + 1):
            for d in range(2):
                for part in parts_of(d, k):
                    arrive(d, k, part)

    def direct(peers, view, sem):
        copies = []
        for i, device in enumerate(peers):
            copy = remote(view, view, ring_send.at[sem, i], ring_recv.at[sem, i], device)
            copy.start()
            copies.append(copy)
        pending.extend(copies)
        yield
        for copy in copies:
            copy.wait_recv()

    def step(*generators):
        return [g for g in generators if next(g, "end") != "end"]

    w_swap.wait()
    w_mine = w_ref[:, mine_cols].astype(F32)
    w_landed = wland[...].astype(F32)[:wrows]
    top = jnp.where(core == 0, w_mine, w_landed)
    bottom = jnp.where(core == 0, w_landed, w_mine)
    w_chip = jnp.concatenate([top, bottom], axis=0).astype(BF16)
    for ch in range(n_chunk):
        for i in range(2):
            start = ch * CHUNK + i * (CHUNK // 2)
            wbuf[i, z, x, ch] = w_chip[:, start : start + CHUNK // 2]
    x_half = x_chips // 2
    z_half = z_chips // 2

    def along_z(ch):
        return ring(
            z_chips, z, z_plus, z_minus, lambda p: wbuf.at[0, p, :, ch],
            lambda h, p: wbuf.at[0, p, pl.ds(h * x_half, x_half), ch], ch, True,
        )

    def along_x(ch):
        return ring(
            x_chips, x, x_plus, x_minus, lambda p: wbuf.at[1, :, p, ch],
            lambda h, p: wbuf.at[1, pl.ds(h * z_half, z_half), p, ch], n_chunk + ch, True,
        )

    upper = (n_chunk + 1) // 2
    w_gathers = [along_z(ch) for ch in range(n_chunk)] + [along_x(ch) for ch in range(n_chunk)]
    w_gathers.append(direct(x_peers, wbuf.at[0, z, x], 2 * n_chunk))
    w_gathers.append(
        ring(
            z_chips, z, z_plus, z_minus, lambda p: wbuf.at[1, p, x],
            lambda h, p: wbuf.at[1, p, x, pl.ds(h * upper, n_chunk - upper if h else upper)],
            2 * n_chunk + 1, False,
        )
    )
    live_w = set(range(2 * n_chunk + 2))

    def step_one(i):
        if i in live_w and not step(w_gathers[i]):
            live_w.discard(i)

    def step_w(point):
        for i in SCHEDULE.get(point, ()):
            step_one(i)

    step_w(0)
    for copy in kv_swaps:
        copy.wait()
    for hh in range(heads):
        ext[hh, pl.ds(2 * nb, 2 * nb), :, 0:HEAD] = own[:, :, pl.ds(hh * HEAD, HEAD)]
        ext[hh, pl.ds(2 * nb, 2 * nb), :, HEAD:] = own[:, :, pl.ds(kvh + hh * HEAD, HEAD)]

    def slash_copy(hh):
        return remote(
            ext.at[hh, pl.ds(2 * nb, 2 * nb)], ext.at[hh, pl.ds(0, 2 * nb)],
            slash_send.at[hh], slash_recv.at[hh], next_chip,
        )

    for hh in range(heads):
        slash_copy(hh).start()
    for copy in row_copies:
        copy.wait_recv()

    per_head = nv - 1
    pieces = 2 * heads // x_chips
    for zz in range(z_chips):
        hh = zz * x_chips // per_head
        entry = vert_ref[core * heads + hh, 1 + zz * x_chips - hh * per_head + x]
        owner = entry // nb
        cand_out[zz] = row_slots[lax.rem(owner // 2, x_chips), lax.rem(owner, 2), hh]
    cand_copies = [
        post(cand_out.at[wrap(z + d, z_chips)], cand_in.at[z], z_peers[d - 1])
        for d in range(1, z_chips)
    ]

    def first_copy(d):
        return remote(
            first_blk.at[x], first_blk.at[x], first_send.at[d - 1], first_recv, z_peers[d - 1]
        )

    @pl.when(z == 0)
    def _():
        for i in range(pieces):
            piece = x * pieces + i
            cols = pl.ds(pl.multiple_of(lax.rem(piece, 2) * HEAD, 128), HEAD)
            first_blk[x, i] = row_slots[0, 0, piece // 2, :, cols]
        for d in range(1, z_chips):
            first_copy(d).start()

    cand_in[z] = cand_out[z]
    step_w(2)
    for copy in cand_copies:
        copy.wait_recv()

    home_head = chip // per_head
    home_entry = vert_ref[core * heads + home_head, 1 + lax.rem(chip, per_head)]
    chosen = cand_in[home_entry // (2 * nb * x_chips)]
    cut = home_a.shape[2]
    home_a[z, x] = chosen[:cut]
    home_b[z, x] = chosen[cut:]
    a_first = [post(home_a.at[z, x], home_a.at[z, x], device) for device in z_peers]
    b_first = [post(home_b.at[z, x], home_b.at[z, x], device) for device in x_peers]

    @pl.when(z > 0)
    def _():
        first_copy(1).wait_recv()

    first_x = [post(first_blk.at[x], first_blk.at[x], device) for device in x_peers]
    step_w(3)
    for copy in b_first:
        copy.wait_recv()
    b_second = [post(home_b.at[z], home_b.at[z], device) for device in z_peers]
    step_w(4)
    for copy in a_first:
        copy.wait_recv()
    a_second = []
    for h in range(heads):
        bundle = home_a.at[pl.ds(h * (z_chips // heads), z_chips // heads), x]
        a_second += [post(bundle, bundle, device) for device in x_peers]
    step_w(5)
    for copy in first_x:
        copy.wait_recv()
    q_load.wait()
    q_swap.wait()

    scale = math.log2(math.e) / math.sqrt(HEAD)
    local = (NS + 2) * BLK
    listed = per_head * BLK
    local_lane = lax.broadcasted_iota(jnp.int32, (1, local), 1) // BLK
    listed_lane = lax.broadcasted_iota(jnp.int32, (1, listed), 1) // BLK
    tile_row = lax.broadcasted_iota(jnp.int32, (group * BLK, 2 * BLK), 0) % BLK
    tile_col = lax.broadcasted_iota(jnp.int32, (group * BLK, 2 * BLK), 1) - BLK
    future = tile_col > tile_row

    def query_of(hh, b):
        return jnp.concatenate(
            [q_buf[b, :, pl.ds((hh * group + h) * HEAD, HEAD)] for h in range(group)], axis=0
        )

    def scores_of(query, keys, bias):
        return lax.dot_general(
            query, keys, (((1,), (1,)), ((), ())), preferred_element_type=F32
        ) + bias

    def hidden_by(valid):
        return jnp.where(valid, 0.0, -jnp.inf).astype(F32)

    def not_slash(entries, block, offsets):
        seen = entries < block
        for offset in offsets:
            seen = jnp.logical_and(seen, entries != block - offset)
        return seen

    def local_info(hh):
        head = core * heads + hh
        info = jnp.where(local_lane == 0, vert_ref[head, 0], 0)
        for i in range(NS):
            info = jnp.where(local_lane == 2 + i, slash_ref[head, i], info)
        return info

    def listed_info(hh):
        head = core * heads + hh
        info = jnp.zeros((1, listed), jnp.int32)
        for j in range(per_head):
            info = jnp.where(listed_lane == j, vert_ref[head, 1 + j], info)
        return info

    def fetch_first(hh):
        for kv in range(2):
            piece = 2 * hh + kv
            kall[hh, pl.ds(listed, BLK), pl.ds(kv * HEAD, HEAD)] = first_blk[
                piece // pieces, piece % pieces
            ]

    def fetch_listed(hh):
        for j in range(per_head):
            e = hh * per_head + j
            kall[hh, pl.ds(j * BLK, cut), 0 : 2 * HEAD] = home_a[e // x_chips, e % x_chips]
            kall[hh, pl.ds(j * BLK + cut, BLK - cut), 0 : 2 * HEAD] = home_b[
                e // x_chips, e % x_chips
            ]

    def attend(hh, info_listed, info_local, b):
        head = core * heads + hh
        block = chip * (2 * nb) + b
        offsets = [slash_ref[head, i] for i in range(NS)]
        for i in range(NS + 1):
            tile = 2 * nb + b - (0 if i == 0 else offsets[i - 1])
            kall[hh, pl.ds(listed + (1 + i) * BLK, BLK), 0 : 2 * HEAD] = ext[hh, tile]
        first_seen = jnp.logical_and(local_lane == 0, not_slash(info_local, block, offsets))
        bias = jnp.concatenate(
            [
                hidden_by(not_slash(info_listed, block, offsets)),
                hidden_by(
                    jnp.logical_or(
                        first_seen, jnp.logical_and(local_lane > 0, info_local <= block)
                    )
                ),
            ],
            axis=1,
        )
        scores = scores_of(query_of(hh, b), kall[hh, :, 0:HEAD], bias)
        scores = jnp.concatenate(
            [
                scores[:, :listed],
                jnp.where(future, -jnp.inf, scores[:, listed : listed + 2 * BLK]),
                scores[:, listed + 2 * BLK :],
            ],
            axis=1,
        )
        top = jnp.max(scores, axis=1, keepdims=True)
        expo = jnp.exp2((scores - top) * scale).astype(BF16)
        sums = jnp.dot(expo, kall[hh, :, HEAD:], preferred_element_type=F32)
        result = (sums[:, :HEAD] / sums[:, HEAD:]).astype(BF16)
        for h in range(group):
            att[core, b, :, pl.ds((hh * group + h) * HEAD, HEAD)] = result[h * BLK : (h + 1) * BLK]

    for hh in range(heads):
        kall[hh, :, 2 * HEAD :] = jnp.ones((listed + local, HEAD), BF16)
        fetch_first(hh)
    step_w(7)
    for copy in b_second + a_second:
        copy.wait_recv()

    @pl.when(z == 0)
    def _():
        for d in range(1, z_chips):
            first_copy(d).wait_send()

    step_w(8)
    parts = 4
    per_part = 2 * nb // parts
    att_copies = []
    for hh in range(heads):
        slash_copy(hh).wait_recv()
    for hh in range(heads):
        fetch_listed(hh)
        infos = (listed_info(hh), local_info(hh))
        for part in range(parts):
            step_w(9 + hh * parts + part)

            @pl.loop(part * per_part, (part + 1) * per_part, unroll=2)
            def _(b):
                attend(hh, *infos, b)

            view = att.at[
                core, pl.ds(part * per_part, per_part), :, pl.ds(hh * group * HEAD, group * HEAD)
            ]
            copy = remote(
                view, view, att_send.at[hh * parts + part], att_recv.at[hh * parts + part], sibling
            )
            copy.start()
            att_copies.append(copy)
    step_w(17)
    for copy in att_copies:
        copy.wait()

    @pl.when(seg == 0)
    def _():
        away, stay = hid_copies()
        away.wait()
        stay.wait()

    subs = 2 * rows // SUB

    def piece(ch, r):
        return (pl.ds(r * SUB, SUB), pl.ds(ch * CHUNK, CHUNK))

    def up(ch, r, src):
        at, i = piece(ch, r), ch * subs + r
        return remote(src.at[at], yin.at[at], y_send.at[i], y_recv.at[i], y_plus)

    def down(ch, r, src):
        at, i = piece(ch, r), ch * subs + r
        return remote(src.at[at], rin.at[at], r_send.at[i], r_recv.at[i], y_minus)

    sent = [[] for _ in range(n_segment)]

    def hand_on(level, ch, k):
        def value(buf, r):
            return buf[piece(ch, r)].astype(F32)

        def own_delta(r):
            return delta[ch, pl.ds(r * SUB, SUB), :]

        def store(buf, r, result):
            buf[piece(ch, r)] = result.astype(BF16)

        def go(way, r, src):
            way(ch, r, src).start()
            sent[k].append((way, ch, r, src))

        def come(way, r):
            way(ch, r, yout).wait_recv()

        chain, skip01, skip12, skip23 = range(4)
        if (level, k) == (0, 0):
            for r, way in ((skip01, down), (skip12, up), (skip23, up), (chain, up)):
                store(yout, r, value(yin, r) + own_delta(r))
                go(way, r, yout)
        elif (level, k) == (0, 1):
            for r, way in ((skip12, down), (skip01, up)):
                store(eout, r, own_delta(r))
                go(way, r, eout)
        elif (level, k) == (0, 2):
            for r, way in ((skip23, down), (skip12, up)):
                store(eout, r, own_delta(r))
                go(way, r, eout)
        elif (level, k) == (1, 0):
            come(down, skip12)
            store(eout, skip12, value(yout, skip12) + value(rin, skip12))
            go(down, skip12, eout)
        elif (level, k) == (1, 1):
            come(down, skip23)
            store(eout, skip23, own_delta(skip23) + value(rin, skip23))
            go(down, skip23, eout)
            for r in (skip12, skip23, chain):
                come(up, r)
                store(yout, r, value(yin, r) + own_delta(r))
                if r != skip12:
                    go(up, r, yout)
        elif (level, k) == (1, 2):
            come(up, skip01)
            store(eout, skip01, value(yin, skip01) + own_delta(skip01))
            go(up, skip01, eout)
        elif (level, k) == (1, 3):
            come(down, skip01)
            go(down, skip01, rin)
        elif (level, k) == (2, 0):
            come(down, skip23)
            store(eout, skip23, value(yout, skip23) + value(rin, skip23))
            go(down, skip23, eout)
        elif (level, k) == (2, 2):
            come(down, skip01)
            go(down, skip01, rin)
            store(
                yout, skip01, value(rin, skip01) + value(yin, skip01) + own_delta(skip01)
            )
            for r in (skip23, chain):
                come(up, r)
                store(yout, r, value(yin, r) + own_delta(r))
                if r == chain:
                    go(up, r, yout)
        elif (level, k) == (2, 3):
            come(down, skip12)
            go(down, skip12, rin)
            for r in (skip01, skip12):
                come(up, r)
                store(yout, r, value(rin, r) + value(yin, r) + own_delta(r))
        elif (level, k) == (3, 1):
            come(down, skip01)
            store(yout, skip01, value(rin, skip01) + own_delta(skip01))
        elif (level, k) == (3, 2):
            come(down, skip12)
            store(yout, skip12, value(rin, skip12) + own_delta(skip12))
        elif (level, k) == (3, 3):
            come(down, skip23)
            store(yout, skip23, value(rin, skip23) + own_delta(skip23))
            come(up, chain)
            store(yout, chain, value(yin, chain) + own_delta(chain))

    def out_copies(ch):
        cols = pl.ds(pl.multiple_of(ch * CHUNK, 128), CHUNK)
        to = pl.ds(pl.multiple_of(core * half + ch * CHUNK, 128), CHUNK)
        stay = pltpu.make_async_copy(yout.at[own_rows, cols], out_ref.at[:, to], local_sem.at[3 + ch])
        away = remote(
            yout.at[their_rows, cols], out_ref.at[:, to], out_send.at[ch], out_recv.at[ch], sibling
        )
        return stay, away

    def project(ch):
        step_w(18 + ch)
        while ch in live_w or n_chunk + ch in live_w:
            step_one(ch)
            step_one(n_chunk + ch)
        left, right = (
            jnp.concatenate(
                [
                    wbuf[i, k * z_half : (k + 1) * z_half, :, ch].reshape(half, CHUNK // 2)
                    for i in range(2)
                ],
                axis=1,
            )
            for k in range(2)
        )
        delta[ch] = jnp.dot(
            att[0].reshape(2 * rows, half), left, preferred_element_type=F32
        ) + jnp.dot(att[1].reshape(2 * rows, half), right, preferred_element_type=F32)

    for t in range(n_chunk + LEVELS - 1):
        if t < n_chunk:
            project(t)
        for level in range(LEVELS):
            ch = t - level
            if 0 <= ch < n_chunk:
                for k in range(n_segment):
                    pl.when(seg == k)(functools.partial(hand_on, level, ch, k))
                if level == LEVELS - 1:
                    for copy in out_copies(ch):
                        copy.start()

    for ch in range(n_chunk):
        for copy in out_copies(ch):
            copy.wait()

    for k in range(n_segment):
        @pl.when(seg == k)
        def _():
            for way, ch, r, src in sent[k]:
                way(ch, r, src).wait_send()

    for copy in pending + [slash_copy(hh) for hh in range(heads)]:
        copy.wait_send()


def on_device(x_chips, n_segment, queries, keys, values, out_proj, hidden_in, vertical, slash):
    row_count = queries.shape[1]
    nb = row_count // BLK
    dq = queries.shape[2]
    dkv = keys.shape[2]
    nv = vertical.shape[2]
    group = dq // dkv
    half = dq // 2
    kvh = dkv // 2
    heads = kvh // HEAD
    wrows = out_proj.shape[1]
    chips = lax.axis_size("seq") // 2
    z_chips = chips // x_chips
    n_chunk = half // CHUNK
    subs = 2 * row_count // SUB
    n_post = 1 + 3 * (z_chips - 1) + (4 + heads) * (x_chips - 1)
    wpad = (wrows + 15) // 16 * 16
    dma = pltpu.SemaphoreType.DMA
    any_space = pl.BlockSpec(memory_space=pl.ANY)
    smem = pl.BlockSpec(memory_space=pltpu.SMEM)
    vmem = pl.BlockSpec(memory_space=pltpu.VMEM)
    out = pl.pallas_call(
        functools.partial(kernel, x_chips, n_segment, nv, group),
        out_shape=jax.ShapeDtypeStruct((row_count, dq), BF16),
        in_specs=[any_space, any_space, any_space, vmem, any_space, smem, smem],
        out_specs=any_space,
        scratch_shapes=[
            pltpu.VMEM((2 * nb, BLK, half), BF16),
            pltpu.VMEM((nb, BLK, dkv), BF16),
            pltpu.VMEM((nb, BLK, dkv), BF16),
            pltpu.VMEM((2, heads, BLK, 2 * HEAD), BF16),
            pltpu.VMEM((2 * nb, BLK, 2 * kvh), BF16),
            pltpu.VMEM((heads, 4 * nb, BLK, 2 * HEAD), BF16),
            pltpu.VMEM((x_chips, 2, heads, BLK, 2 * HEAD), BF16),
            pltpu.VMEM((z_chips, BLK, 2 * HEAD), BF16),
            pltpu.VMEM((z_chips, BLK, 2 * HEAD), BF16),
            pltpu.VMEM((z_chips, x_chips, 48, 2 * HEAD), BF16),
            pltpu.VMEM((z_chips, x_chips, 16, 2 * HEAD), BF16),
            pltpu.VMEM((x_chips, 2 * heads // x_chips, BLK, HEAD), BF16),
            pltpu.VMEM((2, z_chips, x_chips, n_chunk, 2 * wrows, CHUNK // 2), BF16),
            pltpu.VMEM((wpad, half), BF16),
            pltpu.VMEM((wpad, half), BF16),
            pltpu.VMEM((heads, (nv + NS + 1) * BLK, 3 * HEAD), BF16),
            pltpu.VMEM((2, 2 * nb, BLK, half), BF16),
            pltpu.VMEM((2 * row_count, half), BF16),
            pltpu.VMEM((2 * row_count, half), BF16),
            pltpu.VMEM((2 * row_count, half), BF16),
            pltpu.VMEM((2 * row_count, half), BF16),
            pltpu.VMEM((n_chunk, 2 * row_count, CHUNK), F32),
            dma((5,)),
            dma((5,)),
            dma((3 + n_chunk,)),
            dma,
            dma((2 * n_chunk + 2, 16)),
            dma((2 * n_chunk + 2, 16)),
            dma((n_post,)),
            dma((n_post,)),
            dma((heads,)),
            dma((heads,)),
            dma((z_chips - 1,)),
            dma,
            dma((heads * 4,)),
            dma((heads * 4,)),
            dma((n_chunk * subs,)),
            dma((n_chunk * subs,)),
            dma((n_chunk * subs,)),
            dma((n_chunk * subs,)),
            dma((n_chunk,)),
            dma((n_chunk,)),
        ],
        compiler_params=pltpu.CompilerParams(
            collective_id=0, has_side_effects=True, vmem_limit_bytes=56 * 1024 * 1024
        ),
        name="fused_layer",
    )(
        queries[0].reshape(nb, BLK, dq),
        keys[0].reshape(nb, BLK, dkv),
        values[0].reshape(nb, BLK, dkv),
        out_proj[0],
        hidden_in,
        vertical[0],
        slash[0],
    )
    return out[None]


def solution(mesh, x_chips=X_CHIPS):
    in_specs = (
        P("segment", "seq", None),
        P("segment", "seq", None),
        P("segment", "seq", None),
        P("segment", "seq", None),
        P("seq", None),
        P("segment", None, None),
        P("segment", None, None),
    )
    out_specs = P("segment", "seq", None)
    body = functools.partial(on_device, x_chips, mesh.shape["segment"])
    return jax.shard_map(body, mesh=mesh, in_specs=in_specs, out_specs=out_specs, check_vma=False)
```

```python
import functools
import math

import jax
import jax.numpy as jnp
from jax import lax
from jax.experimental import pallas as pl
from jax.experimental.pallas import tpu as pltpu
from jax.sharding import PartitionSpec as P

HEAD = 128
BLK = 64
NS = 4
X_CHIPS = 4
CHUNK = 256
SUB = 128
SCHEDULE = {
    0: (11,), 2: (10, 11), 3: (11,), 5: (10, 11, 0, 1), 7: (11, 0, 1, 5), 8: (6, 2), 9: (0, 1),
    10: (2, 5, 7), 11: (0, 1, 3), 12: (2, 6, 5, 0), 13: (3, 8, 1, 4), 14: (2, 7, 6), 15: (3, 4, 9),
    16: (2, 8, 7), 17: (3, 4), 19: (4, 9),
}
LEVELS = 4
BF16 = jnp.bfloat16
F32 = jnp.float32


def wrap(index, size):
    return lax.rem(index + size, size)


def kernel(
    x_chips, n_segment, nv, group,
    q_ref, k_ref, v_ref, w_ref, hid_ref, vert_ref, slash_ref, out_ref,
    q_buf, k_own, v_own, picked, own, ext, row_slots, cand_out, cand_in, homes, first_blk, wbuf, wsend, wland, kall, att, yin, rin, yout, eout, delta,
    swap_send, swap_recv, local_sem, hid_sem, ring_send, ring_recv, post_send, post_recv,
    slash_send, slash_recv, first_send, first_recv, att_send, att_recv, y_send, y_recv, r_send, r_recv, out_send, out_recv,
):
    seq = lax.axis_index("seq")
    seg = lax.axis_index("segment")
    chips = lax.axis_size("seq") // 2
    z_chips = chips // x_chips
    core = lax.rem(seq, 2)
    other = 1 - core
    chip = seq // 2
    z = chip // x_chips
    x = lax.rem(chip, x_chips)
    nb = k_ref.shape[0]
    rows = nb * BLK
    half = q_ref.shape[2] // 2
    kvh = k_ref.shape[2] // 2
    heads = kvh // HEAD
    n_chunk = half // CHUNK
    wrows = w_ref.shape[0]

    def at_chip(index):
        return {"seq": index * 2 + core}

    sibling = {"seq": chip * 2 + other}
    x_plus = at_chip(z * x_chips + wrap(x + 1, x_chips))
    x_minus = at_chip(z * x_chips + wrap(x - 1, x_chips))
    z_plus = at_chip(wrap(z + 1, z_chips) * x_chips + x)
    z_minus = at_chip(wrap(z - 1, z_chips) * x_chips + x)
    next_chip = at_chip(wrap(chip + 1, chips))
    prev_chip = at_chip(wrap(chip - 1, chips))
    y_plus = {"segment": wrap(seg + 1, n_segment)}
    y_minus = {"segment": wrap(seg - 1, n_segment)}

    def remote(src, dst, send_sem, recv_sem, device):
        return pltpu.make_async_remote_copy(
            src_ref=src, dst_ref=dst, send_sem=send_sem, recv_sem=recv_sem,
            device_id=device, device_id_type=pl.DeviceIdType.MESH,
        )

    barrier = pltpu.get_barrier_semaphore()
    z_peers = [at_chip(wrap(z + d, z_chips) * x_chips + x) for d in range(1, z_chips)]
    x_peers = [at_chip(z * x_chips + wrap(x + d, x_chips)) for d in range(1, x_chips)]
    x_cross = [
        {"seq": (z * x_chips + wrap(x + d, x_chips)) * 2 + other} for d in range(1, x_chips)
    ]
    greeted = [sibling, next_chip, prev_chip, y_plus, y_minus] + z_peers + x_peers + x_cross
    for device in greeted:
        pl.semaphore_signal(barrier, inc=1, device_id=device, device_id_type=pl.DeviceIdType.MESH)

    mine_kv = pl.ds(pl.multiple_of(core * kvh, 128), kvh)
    their_kv = pl.ds(pl.multiple_of(other * kvh, 128), kvh)
    mine_cols = pl.ds(pl.multiple_of(core * half, 128), half)
    their_cols = pl.ds(pl.multiple_of(other * half, 128), half)
    own_blocks = pl.ds(core * nb, nb)
    own_rows = pl.ds(pl.multiple_of(core * rows, 16), rows)
    their_rows = pl.ds(pl.multiple_of(other * rows, 16), rows)

    k_load = pltpu.make_async_copy(k_ref, k_own, local_sem.at[0])
    v_load = pltpu.make_async_copy(v_ref, v_own, local_sem.at[1])
    q_load = pltpu.make_async_copy(q_ref.at[:, :, mine_cols], q_buf.at[own_blocks], local_sem.at[2])
    for copy in (k_load, v_load, q_load):
        copy.start()

    w_theirs = w_ref[:, their_cols].astype(F32)
    pad = wsend.shape[0] - wrows
    if pad:
        w_theirs = jnp.concatenate([w_theirs, jnp.zeros((pad, half), F32)], axis=0)
    wsend[...] = w_theirs.astype(BF16)

    k_load.wait()
    v_load.wait()
    for head in range(2 * heads):
        pick = jnp.int32(0)
        for j in range(nv):
            entry = vert_ref[head, j]
            pick += jnp.where(entry // nb == seq, lax.rem(entry, nb), 0)
        picked[head // heads, head % heads, :, 0:HEAD] = k_own[pick, :, pl.ds(head * HEAD, HEAD)]
        picked[head // heads, head % heads, :, HEAD:] = v_own[pick, :, pl.ds(head * HEAD, HEAD)]
    row_slots[x, core] = picked[core]
    own[own_blocks, :, pl.ds(0, kvh)] = k_own[:, :, mine_kv]
    own[own_blocks, :, pl.ds(kvh, kvh)] = v_own[:, :, mine_kv]

    pl.semaphore_wait(barrier, len(greeted))

    pending = []
    posted = [0]

    def post(src, dst, device):
        i = posted[0]
        posted[0] += 1
        copy = remote(src, dst, post_send.at[i], post_recv.at[i], device)
        copy.start()
        pending.append(copy)
        return copy

    def swap(i, src, dst):
        copy = remote(src, dst, swap_send.at[i], swap_recv.at[i], sibling)
        copy.start()
        return copy

    row_copies = [post(picked.at[other], row_slots.at[x, core], sibling)]
    for d in range(x_chips - 1):
        row_copies.append(post(picked.at[core], row_slots.at[x, core], x_peers[d]))
        row_copies.append(post(picked.at[other], row_slots.at[x, core], x_cross[d]))
    w_swap = swap(3, wsend, wland)
    kv_swaps = [
        swap(0, k_own.at[:, :, their_kv], own.at[own_blocks, :, pl.ds(0, kvh)]),
        swap(1, v_own.at[:, :, their_kv], own.at[own_blocks, :, pl.ds(kvh, kvh)]),
    ]
    q_swap = swap(2, q_ref.at[:, :, their_cols], q_buf.at[own_blocks])

    def hid_copies():
        away = remote(
            hid_ref.at[:, their_cols], yin.at[own_rows], swap_send.at[4], swap_recv.at[4], sibling
        )
        stay = pltpu.make_async_copy(hid_ref.at[:, mine_cols], yin.at[own_rows], hid_sem)
        return away, stay

    @pl.when(seg == 0)
    def _():
        away, stay = hid_copies()
        away.start()
        stay.start()

    def ring(n, me, plus, minus, whole, part_of, sem, split):
        last = n // 2

        def message(d, k, part, sending):
            sign, device = ((1, plus), (-1, minus))[d]
            out_at = wrap(me - sign * (k - 1), n)
            in_at = wrap(me - sign * k, n)
            send = ring_send.at[sem, d * 8 + (k - 1) * 2 + max(part, 0)]
            recv = ring_recv.at[sem, d * 8 + (k - 1) * 2 + max(part, 0)]
            view = whole if part < 0 else functools.partial(part_of, part)
            place = view(out_at if sending else in_at)
            return remote(place, place, send, recv, device)

        waited = set()

        def arrive(d, k, part):
            if (d, k, part) not in waited:
                waited.add((d, k, part))
                message(d, k, part, False).wait_recv()

        def parts_of(d, k):
            order = [0, 1] if d == 0 else [1, 0]
            if k == last:
                return order[:1]
            return order if split else [-1]

        for k in range(1, last + 1):
            for d in range(2):
                for part in parts_of(d, k):
                    if k > 1:
                        arrive(d, k - 1, part if split else -1)
                    outgoing = message(d, k, part, True)
                    outgoing.start()
                    pending.append(outgoing)
            yield
        for k in range(1, last + 1):
            for d in range(2):
                for part in parts_of(d, k):
                    arrive(d, k, part)

    def direct(peers, view, sem):
        copies = []
        for i, device in enumerate(peers):
            copy = remote(view, view, ring_send.at[sem, i], ring_recv.at[sem, i], device)
            copy.start()
            copies.append(copy)
        pending.extend(copies)
        yield
        for copy in copies:
            copy.wait_recv()

    def step(*generators):
        return [g for g in generators if next(g, "end") != "end"]

    w_swap.wait()
    w_mine = w_ref[:, mine_cols].astype(F32)
    w_landed = wland[...].astype(F32)[:wrows]
    top = jnp.where(core == 0, w_mine, w_landed)
    bottom = jnp.where(core == 0, w_landed, w_mine)
    w_chip = jnp.concatenate([top, bottom], axis=0).astype(BF16)
    for ch in range(n_chunk):
        for i in range(2):
            start = ch * CHUNK + i * (CHUNK // 2)
            wbuf[i, z, x, ch] = w_chip[:, start : start + CHUNK // 2]
    x_half = x_chips // 2
    z_half = z_chips // 2

    def along_z(ch):
        return ring(
            z_chips, z, z_plus, z_minus, lambda p: wbuf.at[0, p, :, ch],
            lambda h, p: wbuf.at[0, p, pl.ds(h * x_half, x_half), ch], ch, True,
        )

    def along_x(ch):
        return ring(
            x_chips, x, x_plus, x_minus, lambda p: wbuf.at[1, :, p, ch],
            lambda h, p: wbuf.at[1, pl.ds(h * z_half, z_half), p, ch], n_chunk + ch, False,
        )

    upper = (n_chunk + 1) // 2
    w_gathers = [along_z(ch) for ch in range(n_chunk)] + [along_x(ch) for ch in range(n_chunk)]
    w_gathers.append(direct(x_peers, wbuf.at[0, z, x], 2 * n_chunk))
    w_gathers.append(
        ring(
            z_chips, z, z_plus, z_minus, lambda p: wbuf.at[1, p, x],
            lambda h, p: wbuf.at[1, p, x, pl.ds(h * upper, n_chunk - upper if h else upper)],
            2 * n_chunk + 1, False,
        )
    )
    live_w = set(range(2 * n_chunk + 2))

    def step_one(i):
        if i in live_w and not step(w_gathers[i]):
            live_w.discard(i)

    def step_w(point):
        for i in SCHEDULE.get(point, ()):
            step_one(i)

    step_w(0)
    for copy in kv_swaps:
        copy.wait()
    for hh in range(heads):
        ext[hh, pl.ds(2 * nb, 2 * nb), :, 0:HEAD] = own[:, :, pl.ds(hh * HEAD, HEAD)]
        ext[hh, pl.ds(2 * nb, 2 * nb), :, HEAD:] = own[:, :, pl.ds(kvh + hh * HEAD, HEAD)]

    def slash_copy(hh):
        return remote(
            ext.at[hh, pl.ds(2 * nb, 2 * nb)], ext.at[hh, pl.ds(0, 2 * nb)],
            slash_send.at[hh], slash_recv.at[hh], next_chip,
        )

    for hh in range(heads):
        slash_copy(hh).start()
    for copy in row_copies:
        copy.wait_recv()

    per_head = nv - 1
    pieces = 2 * heads // x_chips
    for zz in range(z_chips):
        hh = zz * x_chips // per_head
        entry = vert_ref[core * heads + hh, 1 + zz * x_chips - hh * per_head + x]
        owner = entry // nb
        cand_out[zz] = row_slots[lax.rem(owner // 2, x_chips), lax.rem(owner, 2), hh]
    cand_copies = [
        post(cand_out.at[wrap(z + d, z_chips)], cand_in.at[z], z_peers[d - 1])
        for d in range(1, z_chips)
    ]

    def first_copy(d):
        return remote(
            first_blk.at[x], first_blk.at[x], first_send.at[d - 1], first_recv, z_peers[d - 1]
        )

    @pl.when(z == 0)
    def _():
        for i in range(pieces):
            piece = x * pieces + i
            cols = pl.ds(pl.multiple_of(lax.rem(piece, 2) * HEAD, 128), HEAD)
            first_blk[x, i] = row_slots[0, 0, piece // 2, :, cols]
        for d in range(1, z_chips):
            first_copy(d).start()

    cand_in[z] = cand_out[z]
    step_w(2)
    for copy in cand_copies:
        copy.wait_recv()

    home_head = chip // per_head
    home_entry = vert_ref[core * heads + home_head, 1 + lax.rem(chip, per_head)]
    chosen = cand_in[home_entry // (2 * nb * x_chips)]
    homes[z, x] = chosen
    home_z = [post(homes.at[z, x], homes.at[z, x], device) for device in z_peers]

    @pl.when(z > 0)
    def _():
        first_copy(1).wait_recv()

    first_x = [post(first_blk.at[x], first_blk.at[x], device) for device in x_peers]
    step_w(3)
    for copy in home_z:
        copy.wait_recv()
    home_x = []
    for h in range(heads):
        bundle = homes.at[pl.ds(h * (z_chips // heads), z_chips // heads), x]
        home_x += [post(bundle, bundle, device) for device in x_peers]
    step_w(5)
    for copy in first_x:
        copy.wait_recv()
    q_load.wait()
    q_swap.wait()

    scale = math.log2(math.e) / math.sqrt(HEAD)
    local = (NS + 2) * BLK
    listed = per_head * BLK
    local_lane = lax.broadcasted_iota(jnp.int32, (1, local), 1) // BLK
    listed_lane = lax.broadcasted_iota(jnp.int32, (1, listed), 1) // BLK
    tile_row = lax.broadcasted_iota(jnp.int32, (group * BLK, 2 * BLK), 0) % BLK
    tile_col = lax.broadcasted_iota(jnp.int32, (group * BLK, 2 * BLK), 1) - BLK
    future = tile_col > tile_row

    def query_of(hh, b):
        return jnp.concatenate(
            [q_buf[b, :, pl.ds((hh * group + h) * HEAD, HEAD)] for h in range(group)], axis=0
        )

    def scores_of(query, keys, bias):
        return lax.dot_general(
            query, keys, (((1,), (1,)), ((), ())), preferred_element_type=F32
        ) + bias

    def hidden_by(valid):
        return jnp.where(valid, 0.0, -jnp.inf).astype(F32)

    def not_slash(entries, block, offsets):
        seen = entries < block
        for offset in offsets:
            seen = jnp.logical_and(seen, entries != block - offset)
        return seen

    def local_info(hh):
        head = core * heads + hh
        info = jnp.where(local_lane == 0, vert_ref[head, 0], 0)
        for i in range(NS):
            info = jnp.where(local_lane == 2 + i, slash_ref[head, i], info)
        return info

    def listed_info(hh):
        head = core * heads + hh
        info = jnp.zeros((1, listed), jnp.int32)
        for j in range(per_head):
            info = jnp.where(listed_lane == j, vert_ref[head, 1 + j], info)
        return info

    def fetch_first(hh):
        for kv in range(2):
            piece = 2 * hh + kv
            kall[hh, pl.ds(listed, BLK), pl.ds(kv * HEAD, HEAD)] = first_blk[
                piece // pieces, piece % pieces
            ]

    def fetch_listed(hh):
        for j in range(per_head):
            e = hh * per_head + j
            kall[hh, pl.ds(j * BLK, BLK), 0 : 2 * HEAD] = homes[e // x_chips, e % x_chips]

    def attend(hh, info_listed, info_local, b):
        head = core * heads + hh
        block = chip * (2 * nb) + b
        offsets = [slash_ref[head, i] for i in range(NS)]
        for i in range(NS + 1):
            tile = 2 * nb + b - (0 if i == 0 else offsets[i - 1])
            kall[hh, pl.ds(listed + (1 + i) * BLK, BLK), 0 : 2 * HEAD] = ext[hh, tile]
        first_seen = jnp.logical_and(local_lane == 0, not_slash(info_local, block, offsets))
        bias = jnp.concatenate(
            [
                hidden_by(not_slash(info_listed, block, offsets)),
                hidden_by(
                    jnp.logical_or(
                        first_seen, jnp.logical_and(local_lane > 0, info_local <= block)
                    )
                ),
            ],
            axis=1,
        )
        scores = scores_of(query_of(hh, b), kall[hh, :, 0:HEAD], bias)
        scores = jnp.concatenate(
            [
                scores[:, :listed],
                jnp.where(future, -jnp.inf, scores[:, listed : listed + 2 * BLK]),
                scores[:, listed + 2 * BLK :],
            ],
            axis=1,
        )
        top = jnp.max(scores, axis=1, keepdims=True)
        expo = jnp.exp2((scores - top) * scale).astype(BF16)
        sums = jnp.dot(expo, kall[hh, :, HEAD:], preferred_element_type=F32)
        result = (sums[:, :HEAD] / sums[:, HEAD:]).astype(BF16)
        for h in range(group):
            att[core, b, :, pl.ds((hh * group + h) * HEAD, HEAD)] = result[h * BLK : (h + 1) * BLK]

    for hh in range(heads):
        kall[hh, :, 2 * HEAD :] = jnp.ones((listed + local, HEAD), BF16)
        fetch_first(hh)
    step_w(7)
    for copy in home_x:
        copy.wait_recv()

    @pl.when(z == 0)
    def _():
        for d in range(1, z_chips):
            first_copy(d).wait_send()

    step_w(8)
    parts = 4
    per_part = 2 * nb // parts
    att_copies = []
    for hh in range(heads):
        slash_copy(hh).wait_recv()
    for hh in range(heads):
        fetch_listed(hh)
        infos = (listed_info(hh), local_info(hh))
        for part in range(parts):
            step_w(9 + hh * parts + part)

            @pl.loop(part * per_part, (part + 1) * per_part, unroll=2)
            def _(b):
                attend(hh, *infos, b)

            view = att.at[
                core, pl.ds(part * per_part, per_part), :, pl.ds(hh * group * HEAD, group * HEAD)
            ]
            copy = remote(
                view, view, att_send.at[hh * parts + part], att_recv.at[hh * parts + part], sibling
            )
            copy.start()
            att_copies.append(copy)
    step_w(17)
    for copy in att_copies:
        copy.wait()

    @pl.when(seg == 0)
    def _():
        away, stay = hid_copies()
        away.wait()
        stay.wait()

    subs = 2 * rows // SUB

    def piece(ch, r):
        return (pl.ds(r * SUB, SUB), pl.ds(ch * CHUNK, CHUNK))

    def up(ch, r, src):
        at, i = piece(ch, r), ch * subs + r
        return remote(src.at[at], yin.at[at], y_send.at[i], y_recv.at[i], y_plus)

    def down(ch, r, src):
        at, i = piece(ch, r), ch * subs + r
        return remote(src.at[at], rin.at[at], r_send.at[i], r_recv.at[i], y_minus)

    sent = [[] for _ in range(n_segment)]

    def hand_on(level, ch, k):
        def value(buf, r):
            return buf[piece(ch, r)].astype(F32)

        def own_delta(r):
            return delta[ch, pl.ds(r * SUB, SUB), :]

        def store(buf, r, result):
            buf[piece(ch, r)] = result.astype(BF16)

        def go(way, r, src):
            way(ch, r, src).start()
            sent[k].append((way, ch, r, src))

        def come(way, r):
            way(ch, r, yout).wait_recv()

        chain, skip01, skip12, skip23 = range(4)
        if (level, k) == (0, 0):
            for r, way in ((skip01, down), (skip12, up), (skip23, up), (chain, up)):
                store(yout, r, value(yin, r) + own_delta(r))
                go(way, r, yout)
        elif (level, k) == (0, 1):
            for r, way in ((skip12, down), (skip01, up)):
                store(eout, r, own_delta(r))
                go(way, r, eout)
        elif (level, k) == (0, 2):
            for r, way in ((skip23, down), (skip12, up)):
                store(eout, r, own_delta(r))
                go(way, r, eout)
        elif (level, k) == (1, 0):
            come(down, skip12)
            store(eout, skip12, value(yout, skip12) + value(rin, skip12))
            go(down, skip12, eout)
        elif (level, k) == (1, 1):
            come(down, skip23)
            store(eout, skip23, own_delta(skip23) + value(rin, skip23))
            go(down, skip23, eout)
            for r in (skip12, skip23, chain):
                come(up, r)
                store(yout, r, value(yin, r) + own_delta(r))
                if r != skip12:
                    go(up, r, yout)
        elif (level, k) == (1, 2):
            come(up, skip01)
            store(eout, skip01, value(yin, skip01) + own_delta(skip01))
            go(up, skip01, eout)
        elif (level, k) == (1, 3):
            come(down, skip01)
            go(down, skip01, rin)
        elif (level, k) == (2, 0):
            come(down, skip23)
            store(eout, skip23, value(yout, skip23) + value(rin, skip23))
            go(down, skip23, eout)
        elif (level, k) == (2, 2):
            come(down, skip01)
            go(down, skip01, rin)
            store(
                yout, skip01, value(rin, skip01) + value(yin, skip01) + own_delta(skip01)
            )
            for r in (skip23, chain):
                come(up, r)
                store(yout, r, value(yin, r) + own_delta(r))
                if r == chain:
                    go(up, r, yout)
        elif (level, k) == (2, 3):
            come(down, skip12)
            go(down, skip12, rin)
            for r in (skip01, skip12):
                come(up, r)
                store(yout, r, value(rin, r) + value(yin, r) + own_delta(r))
        elif (level, k) == (3, 1):
            come(down, skip01)
            store(yout, skip01, value(rin, skip01) + own_delta(skip01))
        elif (level, k) == (3, 2):
            come(down, skip12)
            store(yout, skip12, value(rin, skip12) + own_delta(skip12))
        elif (level, k) == (3, 3):
            come(down, skip23)
            store(yout, skip23, value(rin, skip23) + own_delta(skip23))
            come(up, chain)
            store(yout, chain, value(yin, chain) + own_delta(chain))

    def out_copies(ch):
        cols = pl.ds(pl.multiple_of(ch * CHUNK, 128), CHUNK)
        to = pl.ds(pl.multiple_of(core * half + ch * CHUNK, 128), CHUNK)
        stay = pltpu.make_async_copy(yout.at[own_rows, cols], out_ref.at[:, to], local_sem.at[3 + ch])
        away = remote(
            yout.at[their_rows, cols], out_ref.at[:, to], out_send.at[ch], out_recv.at[ch], sibling
        )
        return stay, away

    def project(ch):
        step_w(18 + ch)
        while ch in live_w or n_chunk + ch in live_w:
            step_one(ch)
            step_one(n_chunk + ch)
        left, right = (
            jnp.concatenate(
                [
                    wbuf[i, k * z_half : (k + 1) * z_half, :, ch].reshape(half, CHUNK // 2)
                    for i in range(2)
                ],
                axis=1,
            )
            for k in range(2)
        )
        delta[ch] = jnp.dot(
            att[0].reshape(2 * rows, half), left, preferred_element_type=F32
        ) + jnp.dot(att[1].reshape(2 * rows, half), right, preferred_element_type=F32)

    for t in range(n_chunk + LEVELS - 1):
        if t < n_chunk:
            project(t)
        for level in range(LEVELS):
            ch = t - level
            if 0 <= ch < n_chunk:
                for k in range(n_segment):
                    pl.when(seg == k)(functools.partial(hand_on, level, ch, k))
                if level == LEVELS - 1:
                    for copy in out_copies(ch):
                        copy.start()

    for ch in range(n_chunk):
        for copy in out_copies(ch):
            copy.wait()

    for k in range(n_segment):
        @pl.when(seg == k)
        def _():
            for way, ch, r, src in sent[k]:
                way(ch, r, src).wait_send()

    for copy in pending + [slash_copy(hh) for hh in range(heads)]:
        copy.wait_send()


def on_device(x_chips, n_segment, queries, keys, values, out_proj, hidden_in, vertical, slash):
    row_count = queries.shape[1]
    nb = row_count // BLK
    dq = queries.shape[2]
    dkv = keys.shape[2]
    nv = vertical.shape[2]
    group = dq // dkv
    half = dq // 2
    kvh = dkv // 2
    heads = kvh // HEAD
    wrows = out_proj.shape[1]
    chips = lax.axis_size("seq") // 2
    z_chips = chips // x_chips
    n_chunk = half // CHUNK
    subs = 2 * row_count // SUB
    n_post = 1 + 2 * (z_chips - 1) + (3 + heads) * (x_chips - 1)
    wpad = (wrows + 15) // 16 * 16
    dma = pltpu.SemaphoreType.DMA
    any_space = pl.BlockSpec(memory_space=pl.ANY)
    smem = pl.BlockSpec(memory_space=pltpu.SMEM)
    vmem = pl.BlockSpec(memory_space=pltpu.VMEM)
    out = pl.pallas_call(
        functools.partial(kernel, x_chips, n_segment, nv, group),
        out_shape=jax.ShapeDtypeStruct((row_count, dq), BF16),
        in_specs=[any_space, any_space, any_space, vmem, any_space, smem, smem],
        out_specs=any_space,
        scratch_shapes=[
            pltpu.VMEM((2 * nb, BLK, half), BF16),
            pltpu.VMEM((nb, BLK, dkv), BF16),
            pltpu.VMEM((nb, BLK, dkv), BF16),
            pltpu.VMEM((2, heads, BLK, 2 * HEAD), BF16),
            pltpu.VMEM((2 * nb, BLK, 2 * kvh), BF16),
            pltpu.VMEM((heads, 4 * nb, BLK, 2 * HEAD), BF16),
            pltpu.VMEM((x_chips, 2, heads, BLK, 2 * HEAD), BF16),
            pltpu.VMEM((z_chips, BLK, 2 * HEAD), BF16),
            pltpu.VMEM((z_chips, BLK, 2 * HEAD), BF16),
            pltpu.VMEM((z_chips, x_chips, BLK, 2 * HEAD), BF16),
            pltpu.VMEM((x_chips, 2 * heads // x_chips, BLK, HEAD), BF16),
            pltpu.VMEM((2, z_chips, x_chips, n_chunk, 2 * wrows, CHUNK // 2), BF16),
            pltpu.VMEM((wpad, half), BF16),
            pltpu.VMEM((wpad, half), BF16),
            pltpu.VMEM((heads, (nv + NS + 1) * BLK, 3 * HEAD), BF16),
            pltpu.VMEM((2, 2 * nb, BLK, half), BF16),
            pltpu.VMEM((2 * row_count, half), BF16),
            pltpu.VMEM((2 * row_count, half), BF16),
            pltpu.VMEM((2 * row_count, half), BF16),
            pltpu.VMEM((2 * row_count, half), BF16),
            pltpu.VMEM((n_chunk, 2 * row_count, CHUNK), F32),
            dma((5,)),
            dma((5,)),
            dma((3 + n_chunk,)),
            dma,
            dma((2 * n_chunk + 2, 16)),
            dma((2 * n_chunk + 2, 16)),
            dma((n_post,)),
            dma((n_post,)),
            dma((heads,)),
            dma((heads,)),
            dma((z_chips - 1,)),
            dma,
            dma((heads * 4,)),
            dma((heads * 4,)),
            dma((n_chunk * subs,)),
            dma((n_chunk * subs,)),
            dma((n_chunk * subs,)),
            dma((n_chunk * subs,)),
            dma((n_chunk,)),
            dma((n_chunk,)),
        ],
        compiler_params=pltpu.CompilerParams(
            collective_id=0, has_side_effects=True, vmem_limit_bytes=56 * 1024 * 1024
        ),
        name="fused_layer",
    )(
        queries[0].reshape(nb, BLK, dq),
        keys[0].reshape(nb, BLK, dkv),
        values[0].reshape(nb, BLK, dkv),
        out_proj[0],
        hidden_in,
        vertical[0],
        slash[0],
    )
    return out[None]


def solution(mesh, x_chips=X_CHIPS):
    in_specs = (
        P("segment", "seq", None),
        P("segment", "seq", None),
        P("segment", "seq", None),
        P("segment", "seq", None),
        P("seq", None),
        P("segment", None, None),
        P("segment", None, None),
    )
    out_specs = P("segment", "seq", None)
    body = functools.partial(on_device, x_chips, mesh.shape["segment"])
    return jax.shard_map(body, mesh=mesh, in_specs=in_specs, out_specs=out_specs, check_vma=False)
```
